256 devices in a mesh: segment: 2 (over x_lo), ha: 8 (over y, core), wa: 16 (over z, x_hi).
Axes of the slice: x: 4 (x_hi: 2, x_lo: 2; x = x_hi * 2 + x_lo), y: 4, z: 8, core: 2. Of those that a mesh axis runs over, the one named last changes fastest.
Arguments:
- latent: bfloat16 [4, 32, 320, 384], P(None, 'ha', 'wa'), may hold values from -6 to 6
- w_mid: bfloat16 [2, 3, 3, 3, 384, 384], P('segment'), may hold values from -0.0625 to 0.0625
- b_mid: float32 [2, 384], P('segment'), may hold values from -1 to 1
- g_mid: float32 [2, 384], P('segment'), may hold values from 0.25 to 1.75
- cache_mid: bfloat16 [2, 2, 32, 320, 384], P('segment', None, 'ha', 'wa'), may hold values from -4 to 4
- w_up: bfloat16 [3, 3, 384, 192], replicated, may hold values from -0.109375 to 0.109375
- b_up: float32 [192], replicated, may hold values from -1 to 1
- g_fine: float32 [192], replicated, may hold values from 0.25 to 1.75
- cache_fine: bfloat16 [2, 64, 640, 192], P(None, 'ha', 'wa'), may hold values from -4 to 4
- w_fine: bfloat16 [3, 3, 3, 192, 192], replicated, may hold values from -0.078125 to 0.078125
- b_fine: float32 [192], replicated, may hold values from -1 to 1
Outputs:
- decoded: bfloat16 [4, 64, 640, 192], P('segment', 'ha', 'wa')
The draws below stay inside these ranges and needn't reach their ends.
All inputs are finite; a program needn't handle non-finite values.
Results may differ from the reference program's by a relative error of at most 0.019.
Values may be sent and summed in bfloat16 or wider, within the bound.
No kernel may reach another device: no remote copies, remote signals or barrier semaphores. Data moves between devices by JAX's collectives and lax.ppermute only.
A program may use at most 128 MiB of HBM per device.

```python
import jax
import jax.numpy as jnp
from jax import lax

CM = 384
CF = 192
FRAMES = 4
ROWS = 32
COLS = 320
FINE_ROWS = 64
FINE_COLS = 640
N_SEGMENT = 2


def shard_levels(rng, dims, split, least, high):
    loudness = 1.0
    for axis_at, parts in split:
        draws = jax.random.uniform(jax.random.fold_in(jax.random.fold_in(rng, 6), axis_at), (parts,), jnp.float32, least / len(split), high / len(split))
        loudness = loudness * jnp.repeat(jnp.exp(draws), dims[axis_at] // parts).reshape((-1,) + (1,) * (len(dims) - 1 - axis_at))
    return loudness


def scatter_about(key, shape, scale, bound, pieces=(), kind=jnp.bfloat16):
    values = jax.random.normal(key, shape, jnp.float32) * scale
    if len(pieces) > 0:
        values = shard_levels(key, shape, pieces, -0.22, 0.18) * values
    return jnp.clip(values, min=-bound, max=bound).astype(kind)


def setup_inputs(seed: int = 0) -> dict:
    keys = jax.random.split(jax.random.key(seed), 12)
    latent = scatter_about(keys[0], (FRAMES, ROWS, COLS, CM), 1.0, 6.0, ((1, 8), (2, 16)))
    w_mid = scatter_about(keys[1], (N_SEGMENT, 3, 3, 3, CM, CM), (27 * CM) ** -0.5, 0.0625, ((0, 2),))
    b_mid = scatter_about(keys[2], (N_SEGMENT, CM), 0.2, 1.0, ((0, 2),), jnp.float32)
    g_mid = jnp.clip(1.0 + 0.15 * jax.random.normal(keys[3], (N_SEGMENT, CM), jnp.float32), 0.25, 1.75)
    cache_mid = scatter_about(keys[4], (N_SEGMENT, 2, ROWS, COLS, CM), 0.6, 4.0, ((0, 2), (2, 8), (3, 16)))
    w_up = scatter_about(keys[5], (3, 3, CM, CF), (9 * CM) ** -0.5, 0.109375)
    b_up = scatter_about(keys[6], (CF,), 0.2, 1.0, (), jnp.float32)
    g_fine = jnp.clip(1.0 + 0.15 * jax.random.normal(keys[7], (CF,), jnp.float32), 0.25, 1.75)
    cache_fine = scatter_about(keys[8], (2, FINE_ROWS, FINE_COLS, CF), 0.6, 4.0, ((1, 8), (2, 16)))
    w_fine = scatter_about(keys[9], (3, 3, 3, CF, CF), (27 * CF) ** -0.5, 0.078125)
    b_fine = scatter_about(keys[10], (CF,), 0.2, 1.0, (), jnp.float32)
    return {"latent": latent, "w_mid": w_mid, "b_mid": b_mid, "g_mid": g_mid, "cache_mid": cache_mid, "w_up": w_up, "b_up": b_up, "g_fine": g_fine, "cache_fine": cache_fine, "w_fine": w_fine, "b_fine": b_fine}


def normed(values, gain_vec):
    as_float = values.astype(jnp.float32)
    inv_rms = lax.rsqrt(lax.optimization_barrier(jnp.mean(as_float * as_float, axis=-1, keepdims=True)) + 1e-06)
    return jax.nn.silu(as_float * inv_rms * gain_vec.astype(jnp.float32)).astype(jnp.bfloat16)

def causal(frames_in, cache_frames, kernel, bias_vec):
    sequence = jnp.concatenate([cache_frames, frames_in], axis=0)
    result = lax.conv_general_dilated(sequence[None], kernel, (1, 1, 1), [(0, 0), (1, 1), (1, 1)], dimension_numbers=('NDHWC', 'DHWIO', 'NDHWC'), preferred_element_type=jnp.float32)[0]
    return result + bias_vec.astype(jnp.float32)

def reference(latent, w_mid, b_mid, g_mid, cache_mid, w_up, b_up, g_fine, cache_fine, w_fine, b_fine):
    section_one = (latent.astype(jnp.float32) + causal(normed(latent, g_mid[0]), cache_mid[0], w_mid[0], b_mid[0])).astype(jnp.bfloat16)
    section_two = (section_one.astype(jnp.float32) + causal(normed(section_one, g_mid[1]), cache_mid[1], w_mid[1], b_mid[1])).astype(jnp.bfloat16)
    doubled = jnp.repeat(jnp.repeat(section_two, 2, axis=1), 2, axis=2)
    upsampled = lax.conv_general_dilated(doubled, w_up, (1, 1), [(1, 1), (1, 1)], dimension_numbers=('NHWC', 'HWIO', 'NHWC'), preferred_element_type=jnp.float32)
    upsampled = (upsampled + b_up.astype(jnp.float32)).astype(jnp.bfloat16)
    fine_input = normed(upsampled, g_fine)
    return (upsampled.astype(jnp.float32) + causal(fine_input, cache_fine, w_fine, b_fine)).astype(jnp.bfloat16)
```

```python
import jax
import jax.numpy as jnp
from jax import lax
from jax.experimental import pallas as pl
from jax.experimental.pallas import tpu as pltpu
from jax.sharding import PartitionSpec as P

F32 = jnp.float32
BF16 = jnp.bfloat16
CM = 384
CF = 192
AXES = ("segment", "ha", "wa")
N_HA = 8
N_WA = 16
GRID_ROWS = 32
GRID_COLS = 320
TILE_ROWS = 4
TILE_COLS = 20
WIDE = 26
NARROW = 24
HALF = 56


def normed(values, gain_vec, channels):
    inv_rms = lax.rsqrt(jnp.sum(values * values, axis=-1, keepdims=True) * (1.0 / channels) + 1e-06)
    scaled = values * inv_rms * gain_vec
    return scaled / (1.0 + jnp.exp(-scaled))


def conv_frames(patches, w_ref, length):
    total = None
    for a in range(3):
        for pq in range(9):
            lhs = patches[a : a + 2, pq].reshape(2 * length, patches.shape[-1])
            part = jnp.dot(lhs, w_ref[a * 9 + pq], preferred_element_type=F32)
            total = part if total is None else total + part
    return total


def first_kernel(group, info, latent, cache, below, left, right, w, b, g, out, raw, act, side, patches):
    @pl.when(info[0] == 0)
    def _():
        last = info[1] == N_HA - 1
        side[0] = left[...].astype(F32)
        side[1] = right[...].astype(F32)
        slots = [(1, False), (2, False), (3, False), (4, True), (3, True), (4, False), (5, False), (6, False)]
        for f in range(4):
            lead = group == 0 and f < 2
            frame = f if group == 1 else (4 + f if lead else f - 2)
            for slot, (row, hide) in enumerate(slots):
                if row >= TILE_ROWS:
                    mid = below[frame, row - TILE_ROWS]
                elif frame >= 4:
                    mid = cache[frame - 4, row]
                else:
                    mid = latent[frame, row]
                mid = mid.astype(F32)
                at = (frame * 7 + row) * 3
                lo = side[0, at : at + 3]
                hi = side[1, at : at + 3]
                if hide:
                    mid = jnp.where(last, 0.0, mid)
                    lo = jnp.where(last, 0.0, lo)
                    hi = jnp.where(last, 0.0, hi)
                base = slot * WIDE
                raw[f, base : base + 3] = lo
                raw[f, base + 3 : base + 3 + TILE_COLS] = mid
                raw[f, base + 3 + TILE_COLS : base + WIDE] = hi
            raw[f, 8 * WIDE : 216] = jnp.zeros((8, CM), F32)
            for h in range(3):
                part = raw[f, h * 72 : h * 72 + 72]
                act[f, h * 72 : h * 72 + 72] = part if lead else normed(part, g[...], CM)
            for p in range(3):
                for q in range(3):
                    top = p * WIDE + q
                    low = top + 4 * WIDE
                    both = jnp.concatenate([act[f, top : top + HALF], act[f, low : low + HALF]], axis=0)
                    patches[f, p * 3 + q] = both.astype(BF16)
        total = conv_frames(patches, w, 2 * HALF) + b[...]
        cols = lax.broadcasted_iota(jnp.int32, (NARROW, 1), 0) + (info[2] * TILE_COLS - 2)
        inside = (cols >= 0) & (cols < GRID_COLS)
        act[0, 0 : 2 * HALF] = total[: 2 * HALF]
        act[1, 0 : 2 * HALF] = total[2 * HALF :]
        for t in range(2):
            for r in range(4):
                src = (r // 2) * HALF + (r % 2) * WIDE
                res = ((r // 2) * 4 + r % 2 + 1) * WIDE + 1
                value = act[t, src : src + NARROW] + raw[2 + t, res : res + NARROW]
                out[t, r] = jnp.where(inside, value, 0.0).astype(BF16)


def second_kernel(group, info, cache, above, top_a, low_a, top_b, low_b, w, b, g, out, raw, act, patches):
    @pl.when(info[0] == 1)
    def _():
        first = info[1] == 0
        last = info[1] == N_HA - 1
        for f in range(4):
            lead = group == 0 and f < 2
            index = f % 2
            top, low = (top_a, low_a) if (group == 0 or f < 2) else (top_b, low_b)
            for u in range(8):
                if lead:
                    row = above[index, u] if u < 2 else cache[index, u - 2]
                else:
                    row = top[index, u] if u < 4 else low[index, u - 4]
                row = row.astype(F32)
                if u < 2:
                    row = jnp.where(first, 0.0, row)
                if u > 5:
                    row = jnp.where(last, 0.0, row)
                raw[f, u * NARROW : (u + 1) * NARROW] = row
            raw[f, 8 * NARROW : 200] = jnp.zeros((8, CM), F32)
            for h in range(2):
                lo, hi = (0, 96) if h == 0 else (96, 200)
                part = raw[f, lo:hi]
                act[f, lo:hi] = part if lead else normed(part, g[...], CM)
            for p in range(3):
                for q in range(3):
                    at = p * NARROW + q
                    patches[f, p * 3 + q] = act[f, at : at + 144].astype(BF16)
        total = conv_frames(patches, w, 144) + b[...]
        cell = lax.broadcasted_iota(jnp.int32, (NARROW, 1), 0)
        cols = cell + (info[2] * TILE_COLS - 1)
        inside = (cols >= 0) & (cols < GRID_COLS) & (cell < 22)
        for t in range(2):
            for i in range(6):
                row_at = info[1] * TILE_ROWS - 1 + i
                fits = inside & (row_at >= 0) & (row_at < GRID_ROWS)
                res = (i + 1) * NARROW + 1
                value = total[t * 144 + i * NARROW : t * 144 + (i + 1) * NARROW] + raw[2 + t, res : res + NARROW]
                out[t, i * NARROW : (i + 1) * NARROW] = jnp.where(fits, value, 0.0).astype(BF16)


def fine_kernel(info, lead, main, returned, cache, w_up, b_up, g, w, b, out, coarse, ups, act, rows, patches, wide):
    def upsample(src, slot, keep):
        for t in range(2):
            coarse[t, 0:144] = src[t].astype(F32)
            coarse[t, 144:160] = jnp.zeros((16, CM), F32)
        lhs = [
            jnp.concatenate([coarse[t, du * NARROW + dv : du * NARROW + dv + 128].astype(BF16) for t in range(2)], axis=0)
            for du in range(2)
            for dv in range(2)
        ]
        cell = lax.broadcasted_iota(jnp.int32, (128, 1), 0)
        col = lax.rem(cell, NARROW)
        for phase in range(4):
            br, bc = phase // 2, phase % 2
            total = None
            for k in range(4):
                part = jnp.dot(lhs[k], w_up[k, :, phase * 256 : phase * 256 + 256], preferred_element_type=F32)
                total = part if total is None else total + part
            value = (total + b_up[...]).astype(BF16).astype(F32)
            if br == 0:
                outside = (cell < NARROW) & (info[1] == 0)
            else:
                outside = (cell >= 4 * NARROW) & (info[1] == N_HA - 1)
            if bc == 0:
                outside |= (col == 0) & (info[2] == 0)
            else:
                outside |= (col == TILE_COLS) & (info[2] == N_WA - 1)
            unit = normed(value, g[...], CF)
            for t in range(2):
                if keep:
                    ups[t, phase] = value[t * 128 : t * 128 + 128]
                act[slot + t, phase] = jnp.where(outside, 0.0, unit[t * 128 : t * 128 + 128])

    @pl.when(info[0] == 0)
    def _():
        for t in range(2):
            for e in range(10):
                line = cache[t, e].astype(F32)
                rows[0, 0:42] = line[:, :128]
                rows[1, 0:42, 0:64] = line[:, 128:]
                br, u = e % 2, e // 2
                for bc in range(2):
                    for c in range(2):
                        act[t, br * 2 + bc, u * NARROW : (u + 1) * NARROW, c * 128 : c * 128 + 128] = rows[
                            c, pl.ds(bc, NARROW, 2), :
                        ]
        upsample(returned, 2, True)

    @pl.when(info[0] == 1)
    def _():
        upsample(lead, 0, False)
        upsample(main, 2, True)

    for f in range(4):
        for plane in range(4):
            for s in range(4):
                at = (s // 2) * NARROW + s % 2
                patches[f, plane * 4 + s] = act[f, plane, at : at + 96].astype(BF16)
    for yb in range(2):
        for xb in range(2):
            total = None
            for a in range(3):
                for p in range(3):
                    for q in range(3):
                        plane = ((yb + p) % 2) * 2 + (xb + q) % 2
                        block = plane * 4 + ((yb + p) // 2) * 2 + (xb + q) // 2
                        lhs = patches[a : a + 2, block].reshape(192, 256)[:, :CF]
                        part = jnp.dot(lhs, w[a * 9 + p * 3 + q], preferred_element_type=F32)
                        total = part if total is None else total + part
            total = total + b[...]
            plane = ((yb + 1) % 2) * 2 + (xb + 1) % 2
            at = ((yb + 1) // 2) * NARROW + (xb + 1) // 2
            for t in range(2):
                value = total[t * 96 : t * 96 + 96] + ups[t, plane, at : at + 96][:, :CF]
                for y in range(4):
                    line = value[y * NARROW : y * NARROW + TILE_COLS]
                    wide[0, t, 2 * y + yb, pl.ds(xb, TILE_COLS, 2), :] = line[:, :128]
                    wide[1, t, 2 * y + yb, pl.ds(xb, TILE_COLS, 2), :] = jnp.concatenate(
                        [line[:, 128:], line[:, 128:]], axis=1
                    )
    for t in range(2):
        for y in range(8):
            out[t, y, :, :128] = wide[0, t, y].astype(BF16)
            out[t, y, :, 128:] = wide[1, t, y][:, :64].astype(BF16)


def call(body, out_shape, scratch, *operands):
    specs = [pl.BlockSpec(memory_space=pltpu.SMEM)] + [pl.BlockSpec(memory_space=pltpu.VMEM)] * (len(operands) - 1)
    return pl.pallas_call(
        body,
        out_shape=jax.ShapeDtypeStruct(out_shape, BF16),
        in_specs=specs,
        out_specs=pl.BlockSpec(memory_space=pltpu.VMEM),
        scratch_shapes=scratch,
        compiler_params=pltpu.CompilerParams(vmem_limit_bytes=40 * 2**20),
    )(*operands)


def device_at(s, h, w):
    return (s * N_HA + h) * N_WA + w


def from_first(by):
    return [
        (device_at(0, (h + by) % N_HA, w), device_at(1, h, w)) for h in range(N_HA) for w in range(N_WA)
    ]


def shards(latent, w_mid, b_mid, g_mid, cache_mid, w_up, b_up, g_fine, cache_fine, w_fine, b_fine):
    segment, ha, wa = (lax.axis_index(axis) for axis in AXES)
    info = jnp.stack([segment, ha, wa]).astype(jnp.int32)
    cache = cache_mid[0]
    kernel = w_mid.reshape(27, CM, CM)

    below = lax.ppermute(
        jnp.concatenate([latent[:, :3], cache[:, :3]], axis=0), "ha", [(i, (i - 1) % N_HA) for i in range(N_HA)]
    )
    tall = jnp.concatenate([jnp.concatenate([latent, cache], axis=0), below], axis=1)
    pad = ((0, 2), (0, 0))
    edge = lambda lo, hi: jnp.pad(tall[:, :, lo:hi].reshape(6 * 7 * 3, CM), pad)
    left = lax.ppermute(edge(TILE_COLS - 3, TILE_COLS), "wa", [(i, i + 1) for i in range(N_WA - 1)])
    right = lax.ppermute(edge(0, 3), "wa", [(i + 1, i) for i in range(N_WA - 1)])

    first_scratch = [
        pltpu.VMEM((4, 216, CM), F32),
        pltpu.VMEM((4, 216, CM), F32),
        pltpu.VMEM((2, 128, CM), F32),
        pltpu.VMEM((4, 9, 2 * HALF, CM), BF16),
    ]
    first = lambda group: call(
        lambda *refs: first_kernel(group, *refs),
        (2, TILE_ROWS, NARROW, CM),
        first_scratch,
        info, latent, cache, below, left, right, kernel, b_mid, g_mid,
    )
    early = first(0)
    low_a, top_a = (lax.ppermute(early, AXES, from_first(by)) for by in (0, -1))
    late = first(1)
    low_b, top_b = (lax.ppermute(late, AXES, from_first(by)) for by in (0, -1))

    sides = [v[:126].reshape(6, 7, 3, CM)[4:, :6] for v in (left, right)]
    cache_ext = jnp.concatenate([sides[0][:, :, 1:], tall[4:, :6], sides[1][:, :, :2]], axis=2)
    above = lax.ppermute(
        cache_ext[:, 2:4],
        AXES,
        [(device_at(1, h, w), device_at(1, h + 1, w)) for h in range(N_HA - 1) for w in range(N_WA)],
    )
    second_scratch = [
        pltpu.VMEM((4, 200, CM), F32),
        pltpu.VMEM((4, 200, CM), F32),
        pltpu.VMEM((4, 9, 144, CM), BF16),
    ]
    second = lambda group: call(
        lambda *refs: second_kernel(group, *refs),
        (2, 6 * NARROW, CM),
        second_scratch,
        info, cache_ext, above, top_a, low_a, top_b, low_b, kernel, b_mid, g_mid,
    )
    second_a = call(
        lambda i, c, ab, ta, la, *refs: second_kernel(0, i, c, ab, ta, la, ta, la, *refs),
        (2, 6 * NARROW, CM),
        second_scratch,
        info, cache_ext, above, top_a, low_a, kernel, b_mid, g_mid,
    )
    returned = lax.ppermute(second_a, "segment", [(1, 0)])
    second_b = call(
        lambda i, ta, la, tb, lb, *refs: second_kernel(1, i, None, None, ta, la, tb, lb, *refs),
        (2, 6 * NARROW, CM),
        second_scratch,
        info, top_a, low_a, top_b, low_b, kernel, b_mid, g_mid,
    )

    fine = cache_fine
    for axis, dim, size in (("ha", 1, N_HA), ("wa", 2, N_WA)):
        up = [(i, i + 1) for i in range(size - 1)]
        down = [(i + 1, i) for i in range(size - 1)]
        length = fine.shape[dim]
        before = lax.ppermute(lax.slice_in_dim(fine, length - 1, length, axis=dim), axis, up)
        after = lax.ppermute(lax.slice_in_dim(fine, 0, 1, axis=dim), axis, down)
        fine = jnp.concatenate([before, fine, after], axis=dim)

    taps = w_up.astype(F32)
    fold = lambda t: jnp.stack([jnp.stack([t[0], t[1] + t[2]]), jnp.stack([t[0] + t[1], t[2]])])
    by_row = [[taps[0], taps[1] + taps[2]], [taps[0] + taps[1], taps[2]]]
    blocks = []
    for du in range(2):
        for dv in range(2):
            places = []
            for br in range(2):
                for bc in range(2):
                    t = by_row[1 - br][du]
                    pair = [[t[0], t[1] + t[2]], [t[0] + t[1], t[2]]][1 - bc][dv]
                    places.append(jnp.pad(pair, ((0, 0), (0, 64))))
            blocks.append(jnp.concatenate(places, axis=1))
    up_kernel = jnp.stack(blocks).astype(BF16)
    lanes = lambda v: jnp.pad(v[None], ((0, 0), (0, 64)))
    return call(
        fine_kernel,
        (2, 8, 40, CF),
        [
            pltpu.VMEM((2, 160, CM), F32),
            pltpu.VMEM((2, 4, 128, 256), F32),
            pltpu.VMEM((4, 4, 128, 256), F32),
            pltpu.VMEM((2, 56, 128), F32),
            pltpu.VMEM((4, 16, 96, 256), BF16),
            pltpu.VMEM((2, 2, 8, 40, 128), F32),
        ],
        info, second_a, second_b, returned, fine, up_kernel, lanes(b_up), lanes(g_fine),
        w_fine.reshape(27, CF, CF), b_fine[None],
    )


def solution(mesh):
    return jax.shard_map(
        shards,
        mesh=mesh,
        in_specs=(
            P(None, "ha", "wa", None),
            P("segment", None, None, None, None, None),
            P("segment", None),
            P("segment", None),
            P("segment", None, "ha", "wa", None),
            P(),
            P(),
            P(),
            P(None, "ha", "wa", None),
            P(),
            P(),
        ),
        out_specs=P("segment", "ha", "wa", None),
        check_vma=False,
    )
```

```python
import jax
import jax.numpy as jnp
from jax import lax
from jax.experimental import pallas as pl
from jax.experimental.pallas import tpu as pltpu
from jax.sharding import PartitionSpec as P

F32 = jnp.float32
BF16 = jnp.bfloat16
CM = 384
CF = 192
AXES = ("segment", "ha", "wa")
N_HA = 8
N_WA = 16
GRID_ROWS = 32
GRID_COLS = 320
ROWS = 4
COLS = 20
PITCH = 24
WIDE = 26
HALF = 56
RING = 2 * 6 * PITCH


def normed(values, gain_vec, channels):
    inv_rms = lax.rsqrt(jnp.sum(values * values, axis=-1, keepdims=True) * (1.0 / channels) + 1e-06)
    scaled = values * inv_rms * gain_vec
    return scaled / (1.0 + jnp.exp(-scaled))


def conv_frames(patches, w, length):
    total = None
    for a in range(3):
        for pq in range(9):
            lhs = patches[a : a + 2, pq].reshape(2 * length, CM)
            part = jnp.dot(lhs, w[a * 9 + pq], preferred_element_type=F32)
            total = part if total is None else total + part
    return total


def frame_pair(first, second):
    return jnp.concatenate([first.astype(F32), second.astype(F32)], axis=1)


def pack_rows(info, latent, cache, fine, to_above, to_below, side):
    def put(at, line):
        side[at : at + line.shape[0]] = line.astype(F32)

    for f in range(2):
        for row in range(3):
            put(((4 + f) * 3 + row) * COLS, cache[f, row])

    @pl.when(info[0] == 0)
    def _():
        for f in range(4):
            for row in range(3):
                put((f * 3 + row) * COLS, latent[f, row])
        to_above[...] = side[...].astype(BF16)

    @pl.when(info[0] == 1)
    def _():
        put(0, frame_pair(fine[0, 0], fine[1, 0]))
        to_above[...] = side[...].astype(BF16)
        for f in range(2):
            for row in range(2):
                put((f * 2 + row) * COLS, cache[f, 2 + row])
        put(80, frame_pair(fine[0, 7], fine[1, 7]))
        to_below[...] = side[0:128].astype(BF16)


def pack_columns(info, latent, cache, fine, below, above, _, left_0, right_0, left_1, right_1, far, side):
    far[0] = below[...].astype(F32)

    @pl.when(info[0] == 0)
    def _():
        for f in range(6):
            for row in range(1, 7):
                if row < ROWS:
                    line = (latent[f, row] if f < 4 else cache[f - 4, row]).astype(F32)
                    first, final = line[:3], line[17:20]
                else:
                    base = (f * 3 + row - ROWS) * COLS
                    first, final = far[0, base : base + 3], far[0, base + 17 : base + 20]
                at = (f * 6 + row - 1) * 3
                side[0, at : at + 3] = first
                side[1, at : at + 3] = final
        left_0[...] = side[0].astype(BF16)
        right_0[...] = side[1].astype(BF16)

    @pl.when(info[0] == 1)
    def _():
        far[1, 0:128] = above[...].astype(F32)
        for t in range(2):
            for u in range(8):
                if 2 <= u < 6:
                    line = cache[t, u - 2].astype(F32)
                    first, final = line[:2], line[18:20]
                else:
                    k, base = (1, (t * 2 + u) * COLS) if u < 2 else (0, ((4 + t) * 3 + u - 6) * COLS)
                    first, final = far[k, base : base + 2], far[k, base + 18 : base + 20]
                at = (t * 8 + u) * 2
                side[0, at : at + 2] = first
                side[1, at : at + 2] = final
        for e in range(10):
            if 1 <= e <= 8:
                line = frame_pair(fine[0, e - 1], fine[1, e - 1])
                first, final = line[0:1], line[39:40]
            else:
                k, base = (1, 80) if e == 0 else (0, 0)
                first, final = far[k, base : base + 1], far[k, base + 39 : base + 40]
            side[0, 32 + e : 33 + e] = first
            side[1, 32 + e : 33 + e] = final
        left_1[...] = side[0, 0:48].astype(BF16)
        right_1[...] = side[1, 0:48].astype(BF16)


def fold_weights(w_up_hbm, w_up, sem, out):
    copy = pltpu.make_async_copy(w_up_hbm, w_up, sem)
    copy.start()
    copy.wait()
    zeros = jnp.zeros((CM, 64), F32)
    taps = [jnp.transpose(w_up[k].astype(F32)) for k in range(9)]
    for br in range(2):
        for bc in range(2):
            place = br * 2 + bc
            for du in range(2):
                ps = ((0, 1), (2,))[du] if br == 0 else ((0,), (1, 2))[du]
                for dv in range(2):
                    qs = ((0, 1), (2,))[dv] if bc == 0 else ((0,), (1, 2))[dv]
                    total = None
                    for p in ps:
                        for q in qs:
                            part = taps[p * 3 + q]
                            total = part if total is None else total + part
                    both = jnp.concatenate([total, zeros], axis=1).astype(BF16)
                    out[du * 2 + dv, :, place * 256 : place * 256 + 256] = both


def first_section(group, info, latent, cache, below, left, right, w, b, g, out, raw, act, side, far, patches):
    last = info[1] == N_HA - 1
    side[0] = left[...].astype(F32)
    side[1] = right[...].astype(F32)
    far[...] = below[...].astype(F32)
    slots = [(1, False), (2, False), (3, False), (4, True), (3, True), (4, False), (5, False), (6, False)]
    for f in range(4):
        lead = group == 0 and f < 2
        frame = f if group == 1 else (4 + f if lead else f - 2)
        for slot, (row, hide) in enumerate(slots):
            if row >= ROWS:
                base = (frame * 3 + row - ROWS) * COLS
                line = far[base : base + COLS]
            else:
                line = (latent[frame, row] if frame < 4 else cache[frame - 4, row]).astype(F32)
            at = (frame * 6 + row - 1) * 3
            before = side[0, at : at + 3]
            after = side[1, at : at + 3]
            if hide:
                line, before, after = (jnp.where(last, 0.0, v) for v in (line, before, after))
            base = slot * WIDE
            raw[f, base : base + 3] = before
            raw[f, base + 3 : base + 3 + COLS] = line
            raw[f, base + 3 + COLS : base + WIDE] = after
        raw[f, 8 * WIDE : 216] = jnp.zeros((8, CM), F32)
        for lo in range(0, 216, 72):
            part = raw[f, lo : lo + 72]
            act[f, lo : lo + 72] = part if lead else normed(part, g[...], CM)
        for p in range(3):
            for q in range(3):
                top = p * WIDE + q
                low = top + 4 * WIDE
                both = jnp.concatenate([act[f, top : top + HALF], act[f, low : low + HALF]], axis=0)
                patches[f, p * 3 + q] = both.astype(BF16)
    total = conv_frames(patches, w, 2 * HALF) + b[...]
    cols = lax.broadcasted_iota(jnp.int32, (PITCH, 1), 0) + (info[2] * COLS - 2)
    inside = (cols >= 0) & (cols < GRID_COLS)
    act[0, 0 : 2 * HALF] = total[: 2 * HALF]
    act[1, 0 : 2 * HALF] = total[2 * HALF :]
    for t in range(2):
        for r in range(4):
            src = (r // 2) * HALF + (r % 2) * WIDE
            res = ((r // 2) * 4 + r % 2 + 1) * WIDE + 1
            value = act[t, src : src + PITCH] + raw[2 + t, res : res + PITCH]
            out[t, r] = jnp.where(inside, value, 0.0).astype(BF16)


def first_early(info, latent, cache, below, left, right, w, b, g, out, *scratch):
    @pl.when(info[0] == 0)
    def _():
        first_section(0, info, latent, cache, below, left, right, w, b, g, out, *scratch)


def first_late(info, latent, below, left, right, w, b, g, w_up_hbm, out, folded, *scratch):
    *scratch, w_up, sems = scratch

    @pl.when(info[0] == 0)
    def _():
        first_section(1, info, latent, None, below, left, right, w, b, g, out, *scratch)

    @pl.when(info[0] == 1)
    def _():
        fold_weights(w_up_hbm, w_up, sems.at[0], folded)


def second_section(info, caches, earlier, later, w, b, g, out, raw, act, side, far, patches):
    first, last = info[1] == 0, info[1] == N_HA - 1
    if caches is not None:
        cache, below, above, left, right = caches
        side[0, 0:48] = left[...].astype(F32)
        side[1, 0:48] = right[...].astype(F32)
        far[0] = below[...].astype(F32)
        far[1, 0:128] = above[...].astype(F32)
    for f in range(4):
        lead = caches is not None and f < 2
        t = f % 2
        for u in range(8):
            base = u * PITCH
            hide = first if u < 2 else (last if u > 5 else None)
            if lead:
                if 2 <= u < 6:
                    line = cache[t, u - 2].astype(F32)
                else:
                    k, at = (1, (t * 2 + u) * COLS) if u < 2 else (0, ((4 + t) * 3 + u - 6) * COLS)
                    line = far[k, at : at + COLS]
                at = (t * 8 + u) * 2
                before = side[0, at : at + 2]
                after = side[1, at : at + 2]
                if hide is not None:
                    line, before, after = (jnp.where(hide, 0.0, v) for v in (line, before, after))
                raw[f, base : base + 2] = before
                raw[f, base + 2 : base + 22] = line
                raw[f, base + 22 : base + 24] = after
            else:
                low, top = earlier if caches is not None or f < 2 else later
                line = (top[t, u] if u < 4 else low[t, u - 4]).astype(F32)
                raw[f, base : base + PITCH] = line if hide is None else jnp.where(hide, 0.0, line)
        raw[f, 8 * PITCH : 200] = jnp.zeros((8, CM), F32)
        for lo, hi in ((0, 96), (96, 200)):
            part = raw[f, lo:hi]
            act[f, lo:hi] = part if lead else normed(part, g[...], CM)
        for p in range(3):
            for q in range(3):
                at = p * PITCH + q
                patches[f, p * 3 + q] = act[f, at : at + 144].astype(BF16)
    total = conv_frames(patches, w, 144) + b[...]
    cell = lax.broadcasted_iota(jnp.int32, (PITCH, 1), 0)
    cols = cell + (info[2] * COLS - 1)
    inside = (cols >= 0) & (cols < GRID_COLS) & (cell < 22)
    for t in range(2):
        for i in range(6):
            row_at = info[1] * ROWS - 1 + i
            fits = inside & (row_at >= 0) & (row_at < GRID_ROWS)
            res = (i + 1) * PITCH + 1
            at = t * 144 + i * PITCH
            value = total[at : at + PITCH] + raw[2 + t, res : res + PITCH]
            out[at : at + PITCH] = jnp.where(fits, value, 0.0).astype(BF16)


def second_early(info, cache, below, above, left, right, low, top, w, b, g, w_up_hbm, out, folded, *scratch):
    *scratch, ring, w_up, sems = scratch

    @pl.when(info[0] == 1)
    def _():
        second_section(info, (cache, below, above, left, right), (low, top), None, w, b, g, out, *scratch)
        first, last = info[1] == 0, info[1] == N_HA - 1
        side, far = scratch[2:4]
        ring[...] = jnp.zeros((112, CM), F32)
        for at, e, line, hide in ((0, 0, far[1, 80:120], first), (48, 9, far[0, 0:40], last)):
            ring[at : at + 1] = jnp.where(hide, 0.0, side[0, 32 + e : 33 + e])
            ring[at + 1 : at + 41] = jnp.where(hide, 0.0, line)
            ring[at + 41 : at + 42] = jnp.where(hide, 0.0, side[1, 32 + e : 33 + e])
        ring[96:104] = side[0, 33:41]
        ring[104:112] = side[1, 33:41]
        out[RING : RING + 112] = ring[...].astype(BF16)

    @pl.when(info[0] == 0)
    def _():
        fold_weights(w_up_hbm, w_up, sems.at[0], folded)


def second_late(info, low_a, top_a, low_b, top_b, w, b, g, out, *scratch):
    @pl.when(info[0] == 1)
    def _():
        second_section(info, None, (low_a, top_a), (low_b, top_b), w, b, g, out, *scratch)


def last_section(info, lead, main, returned, cache, folded_0, folded_1, b_up, g, w_hbm, b,
                 out, coarse, ups, act, rows, ring, patches, wide, w, sems):
    copy = pltpu.make_async_copy(w_hbm, w, sems.at[0])
    copy.start()
    lanes = lambda ref: jnp.concatenate([ref[...], jnp.zeros((1, 64), F32)], axis=1)
    bias, gain = lanes(b_up), lanes(g)

    def upsample(src, w_up, slot, keep):
        for t in range(2):
            coarse[t, 0:144] = src[t * 144 : t * 144 + 144].astype(F32)
            coarse[t, 144:160] = jnp.zeros((16, CM), F32)
        lhs = [
            jnp.concatenate([coarse[t, du * PITCH + dv : du * PITCH + dv + 128].astype(BF16) for t in range(2)], axis=0)
            for du in range(2)
            for dv in range(2)
        ]
        cell = lax.broadcasted_iota(jnp.int32, (128, 1), 0)
        col = lax.rem(cell, PITCH)
        for phase in range(4):
            br, bc = phase // 2, phase % 2
            total = None
            for k in range(4):
                part = jnp.dot(lhs[k], w_up[k, :, phase * 256 : phase * 256 + 256], preferred_element_type=F32)
                total = part if total is None else total + part
            value = (total + bias).astype(BF16).astype(F32)
            if br == 0:
                outside = (cell < PITCH) & (info[1] == 0)
            else:
                outside = (cell >= 4 * PITCH) & (info[1] == N_HA - 1)
            if bc == 0:
                outside |= (col == 0) & (info[2] == 0)
            else:
                outside |= (col == COLS) & (info[2] == N_WA - 1)
            unit = normed(value, gain, CF)
            for t in range(2):
                if keep:
                    ups[t, phase] = value[t * 128 : t * 128 + 128]
                act[slot + t, phase] = jnp.where(outside, 0.0, unit[t * 128 : t * 128 + 128])

    @pl.when(info[0] == 0)
    def _():
        ring[...] = returned[RING : RING + 112].astype(F32)
        for t in range(2):
            part = slice(t * CF, t * CF + CF)
            for e in range(10):
                if e == 0 or e == 9:
                    at = 0 if e == 0 else 48
                    line = ring[at : at + 48][:, part]
                    rows[0, 0:48] = line[:, :128]
                    rows[1, 0:48, 0:64] = line[:, 128:]
                else:
                    line = cache[t, e - 1].astype(F32)
                    rows[0, 1:41] = line[:, :128]
                    rows[1, 1:41, 0:64] = line[:, 128:]
                    for at, col in ((95 + e, 0), (103 + e, 41)):
                        end = ring[at : at + 1][:, part]
                        rows[0, col : col + 1] = end[:, :128]
                        rows[1, col : col + 1, 0:64] = end[:, 128:]
                br, u = e % 2, e // 2
                for bc in range(2):
                    for c in range(2):
                        act[t, br * 2 + bc, u * PITCH : (u + 1) * PITCH, c * 128 : c * 128 + 128] = rows[
                            c, pl.ds(bc, PITCH, 2), :
                        ]
        upsample(returned, folded_0, 2, True)

    @pl.when(info[0] == 1)
    def _():
        upsample(lead, folded_1, 0, False)
        upsample(main, folded_1, 2, True)

    for f in range(4):
        for plane in range(4):
            for s in range(4):
                at = (s // 2) * PITCH + s % 2
                patches[f, plane * 4 + s] = act[f, plane, at : at + 96].astype(BF16)
    copy.wait()
    for yb in range(2):
        for xb in range(2):
            total = None
            for a in range(3):
                for p in range(3):
                    for q in range(3):
                        plane = ((yb + p) % 2) * 2 + (xb + q) % 2
                        block = plane * 4 + ((yb + p) // 2) * 2 + (xb + q) // 2
                        lhs = patches[a : a + 2, block].reshape(192, 256)[:, :CF]
                        part = jnp.dot(lhs, w[a * 9 + p * 3 + q], preferred_element_type=F32)
                        total = part if total is None else total + part
            total = total + b[...]
            plane = ((yb + 1) % 2) * 2 + (xb + 1) % 2
            at = ((yb + 1) // 2) * PITCH + (xb + 1) // 2
            for t in range(2):
                value = total[t * 96 : t * 96 + 96] + ups[t, plane, at : at + 96][:, :CF]
                for y in range(4):
                    line = value[y * PITCH : y * PITCH + COLS]
                    wide[0, t, 2 * y + yb, pl.ds(xb, COLS, 2), :] = line[:, :128]
                    wide[1, t, 2 * y + yb, pl.ds(xb, COLS, 2), :] = jnp.concatenate(
                        [line[:, 128:], line[:, 128:]], axis=1
                    )
    for t in range(2):
        for y in range(8):
            out[t, y, :, :128] = wide[0, t, y].astype(BF16)
            out[t, y, :, 128:] = wide[1, t, y][:, :64].astype(BF16)


VMEM = pl.BlockSpec(memory_space=pltpu.VMEM)
SMEM = pl.BlockSpec(memory_space=pltpu.SMEM)
HBM = pl.BlockSpec(memory_space=pltpu.HBM)


def call(body, specs, outs, scratch, *operands, flops=0, megabytes=20):
    kinds = {"s": SMEM, "v": VMEM, "h": HBM}
    return pl.pallas_call(
        body,
        out_shape=[jax.ShapeDtypeStruct(shape, BF16) for shape in outs],
        in_specs=[kinds[c] for c in specs],
        out_specs=[VMEM] * len(outs),
        scratch_shapes=scratch,
        compiler_params=pltpu.CompilerParams(vmem_limit_bytes=megabytes * 2**20),
        cost_estimate=pl.CostEstimate(flops=flops, bytes_accessed=2**20, transcendentals=0),
    )(*operands)


def device_at(s, h, w):
    return (s * N_HA + h) * N_WA + w


def pairs_between(src_seg, dst_seg, dh, dw, wrap=False):
    pairs = []
    for h in range(N_HA):
        for w in range(N_WA):
            if (wrap or 0 <= h - dh < N_HA) and 0 <= w - dw < N_WA:
                pairs.append((device_at(src_seg, (h - dh) % N_HA, w - dw), device_at(dst_seg, h, w)))
    return pairs


def shards(latent, w_mid, b_mid, g_mid, cache_mid, w_up, b_up, g_fine, cache_fine, w_fine, b_fine):
    info = jnp.stack([lax.axis_index(axis) for axis in AXES]).astype(jnp.int32)
    kernel = w_mid.reshape(27, CM, CM)
    up_kernel = jnp.swapaxes(w_up, 2, 3).reshape(9, CF, CM)
    dma = pltpu.SemaphoreType.DMA

    cache = cache_mid[0]
    side = pltpu.VMEM((2, 112, CM), F32)
    far = lambda count: pltpu.VMEM((count, 368, CM) if count > 1 else (368, CM), F32)
    to_above, to_below = call(
        pack_rows, "svvv", [(368, CM), (128, CM)], [far(1)], info, latent, cache, cache_fine, megabytes=3
    )
    below = lax.ppermute(to_above, "ha", [(i, (i - 1) % N_HA) for i in range(N_HA)])
    above = lax.ppermute(to_below, AXES, pairs_between(1, 1, 1, 0))
    sides = call(
        pack_columns, "svvvvvv", [(112, CM)] * 2 + [(48, CM)] * 2, [far(2), side],
        info, latent, cache, cache_fine, below, above, kernel, megabytes=3,
    )
    right_0, left_0 = (lax.ppermute(sides[k], AXES, pairs_between(0, 0, 0, 2 * k - 1)) for k in range(2))
    right_1, left_1 = (lax.ppermute(sides[2 + k], AXES, pairs_between(1, 1, 0, 2 * k - 1)) for k in range(2))

    up_scratch = [pltpu.VMEM((9, CF, CM), BF16), dma((1,))]
    folded_shape = (4, CM, 1024)
    first_scratch = [
        pltpu.VMEM((4, 216, CM), F32),
        pltpu.VMEM((4, 216, CM), F32),
        side,
        far(1),
        pltpu.VMEM((4, 9, 2 * HALF, CM), BF16),
    ]
    first_shape = (2, ROWS, PITCH, CM)
    first_flops = 2 * 224 * 27 * CM * CM
    spread = lambda tile: [lax.ppermute(tile, AXES, pairs_between(0, 1, dh, 0, True)) for dh in range(2)]
    (early,) = call(
        first_early, "svvvvvvvv", [first_shape], first_scratch,
        info, latent, cache, below, left_0, right_0, kernel, b_mid, g_mid, flops=first_flops, megabytes=16,
    )
    group_a = spread(early)
    late, folded_1 = call(
        first_late, "svvvvvvvh", [first_shape, folded_shape], first_scratch + up_scratch,
        info, latent, below, left_0, right_0, kernel, b_mid, g_mid, up_kernel, flops=first_flops, megabytes=16,
    )
    group_b = spread(late)

    second_scratch = [
        pltpu.VMEM((4, 200, CM), F32),
        pltpu.VMEM((4, 200, CM), F32),
        side,
        far(2),
        pltpu.VMEM((4, 9, 144, CM), BF16),
    ]
    second_flops = 2 * 288 * 27 * CM * CM
    second_a, folded_0 = call(
        second_early, "svvvvvvvvvvh", [(RING + 112, CM), folded_shape],
        second_scratch + [pltpu.VMEM((112, CM), F32)] + up_scratch,
        info, cache, below, above, left_1, right_1, *group_a, kernel, b_mid, g_mid, up_kernel, flops=second_flops, megabytes=16,
    )
    returned = lax.ppermute(second_a, "segment", [(1, 0)])
    (second_b,) = call(
        second_late, "svvvvvvv", [(RING, CM)], second_scratch,
        info, *group_a, *group_b, kernel, b_mid, g_mid, flops=second_flops, megabytes=16,
    )
    (decoded,) = call(
        last_section, "svvvvvvvvhv", [(2, 8, 40, CF)],
        [
            pltpu.VMEM((2, 160, CM), F32),
            pltpu.VMEM((2, 4, 128, 256), F32),
            pltpu.VMEM((4, 4, 128, 256), F32),
            pltpu.VMEM((2, 56, 128), F32),
            pltpu.VMEM((112, CM), F32),
            pltpu.VMEM((4, 16, 96, 256), BF16),
            pltpu.VMEM((2, 2, 8, 40, 128), F32),
            pltpu.VMEM((27, CF, CF), BF16),
            dma((1,)),
        ],
        info, second_a, second_b, returned, cache_fine, folded_0, folded_1,
        b_up[None], g_fine[None], w_fine.reshape(27, CF, CF), b_fine[None],
        flops=2 * 768 * 27 * CF * CF, megabytes=16,
    )
    return decoded


def solution(mesh):
    return jax.shard_map(
        shards,
        mesh=mesh,
        in_specs=(
            P(None, "ha", "wa", None),
            P("segment", None, None, None, None, None),
            P("segment", None),
            P("segment", None),
            P("segment", None, "ha", "wa", None),
            P(),
            P(),
            P(),
            P(None, "ha", "wa", None),
            P(),
            P(),
        ),
        out_specs=P("segment", "ha", "wa", None),
        check_vma=False,
    )
```

```python
import jax
import jax.numpy as jnp
from jax import lax
from jax.experimental import pallas as pl
from jax.experimental.pallas import tpu as pltpu
from jax.sharding import PartitionSpec as P

F32 = jnp.float32
BF16 = jnp.bfloat16
CM = 384
CF = 192
AXES = ("segment", "ha", "wa")
N_HA = 8
N_WA = 16
GRID_ROWS = 32
GRID_COLS = 320
ROWS = 4
COLS = 20
PITCH = 24
WIDE = 26
HALF = 56
RING = 2 * 6 * PITCH


def normed(values, gain_vec, channels):
    inv_rms = lax.rsqrt(jnp.sum(values * values, axis=-1, keepdims=True) * (1.0 / channels) + 1e-06)
    scaled = values * inv_rms * gain_vec
    half = 0.5 * scaled
    return half + half * jnp.tanh(half)


def conv_frames(stores, w):
    total = None
    for a in range(3):
        lhs = jnp.concatenate([stores[a][...], stores[a + 1][...]], axis=0)
        part = jnp.dot(lhs, w[a], preferred_element_type=F32)
        total = part if total is None else total + part
    return total


def frame_pair(first, second):
    return jnp.concatenate([first.astype(F32), second.astype(F32)], axis=1)


def pack_rows(info, latent, cache, fine, to_above, to_below, side):
    def put(at, line):
        side[at : at + line.shape[0]] = line.astype(F32)

    for f in range(2):
        for row in range(3):
            put(((4 + f) * 3 + row) * COLS, cache[f, row])

    @pl.when(info[0] == 0)
    def _():
        for f in range(4):
            for row in range(3):
                put((f * 3 + row) * COLS, latent[f, row])
        to_above[...] = side[...].astype(BF16)

    @pl.when(info[0] == 1)
    def _():
        put(0, frame_pair(fine[0, 0], fine[1, 0]))
        to_above[...] = side[...].astype(BF16)
        for f in range(2):
            for row in range(2):
                put((f * 2 + row) * COLS, cache[f, 2 + row])
        put(80, frame_pair(fine[0, 7], fine[1, 7]))
        to_below[...] = side[0:128].astype(BF16)


def pack_columns(info, latent, cache, fine, below, above, left_0, right_0, left_1, right_1, far, side):
    far[0] = below[...].astype(F32)

    @pl.when(info[0] == 0)
    def _():
        for f in range(6):
            for row in range(1, 7):
                if row < ROWS:
                    line = (latent[f, row] if f < 4 else cache[f - 4, row]).astype(F32)
                    first, final = line[:3], line[17:20]
                else:
                    base = (f * 3 + row - ROWS) * COLS
                    first, final = far[0, base : base + 3], far[0, base + 17 : base + 20]
                at = (f * 6 + row - 1) * 3
                side[0, at : at + 3] = first
                side[1, at : at + 3] = final
        left_0[...] = side[0].astype(BF16)
        right_0[...] = side[1].astype(BF16)

    @pl.when(info[0] == 1)
    def _():
        far[1, 0:128] = above[...].astype(F32)
        for t in range(2):
            for u in range(8):
                if 2 <= u < 6:
                    line = cache[t, u - 2].astype(F32)
                    first, final = line[:2], line[18:20]
                else:
                    k, base = (1, (t * 2 + u) * COLS) if u < 2 else (0, ((4 + t) * 3 + u - 6) * COLS)
                    first, final = far[k, base : base + 2], far[k, base + 18 : base + 20]
                at = (t * 8 + u) * 2
                side[0, at : at + 2] = first
                side[1, at : at + 2] = final
        for e in range(10):
            if 1 <= e <= 8:
                line = frame_pair(fine[0, e - 1], fine[1, e - 1])
                first, final = line[0:1], line[39:40]
            else:
                k, base = (1, 80) if e == 0 else (0, 0)
                first, final = far[k, base : base + 1], far[k, base + 39 : base + 40]
            side[0, 32 + e : 33 + e] = first
            side[1, 32 + e : 33 + e] = final
        left_1[...] = side[0, 0:48].astype(BF16)
        right_1[...] = side[1, 0:48].astype(BF16)


def fold_weights(w_up_hbm, w_up, sem, out):
    copy = pltpu.make_async_copy(w_up_hbm, w_up, sem)
    copy.start()
    copy.wait()
    zeros = jnp.zeros((CM, 64), F32)
    taps = [jnp.transpose(w_up[k].astype(F32)) for k in range(9)]
    for br in range(2):
        for bc in range(2):
            place = br * 2 + bc
            for du in range(2):
                ps = ((0, 1), (2,))[du] if br == 0 else ((0,), (1, 2))[du]
                for dv in range(2):
                    qs = ((0, 1), (2,))[dv] if bc == 0 else ((0,), (1, 2))[dv]
                    total = None
                    for p in ps:
                        for q in qs:
                            part = taps[p * 3 + q]
                            total = part if total is None else total + part
                    both = jnp.concatenate([total, zeros], axis=1).astype(BF16)
                    out[(du * 2 + dv) * CM : (du * 2 + dv + 1) * CM, place * 256 : place * 256 + 256] = both


def first_section(group, info, latent, cache, below, left, right, w, b, g, out, kept, raw, act, side, far, patches):
    stores = [patches.at[0], patches.at[1], kept.at[0], kept.at[1]]
    if group == 1:
        stores = stores[2:] + stores[:2]
    last = info[1] == N_HA - 1
    side[0] = left[...].astype(F32)
    side[1] = right[...].astype(F32)
    far[...] = below[...].astype(F32)
    slots = [(1, False), (2, False), (3, False), (4, True), (3, True), (4, False), (5, False), (6, False)]
    for f in range(2 * group, 4):
        lead = group == 0 and f < 2
        frame = f if group == 1 else (4 + f if lead else f - 2)
        for slot, (row, hide) in enumerate(slots):
            if row >= ROWS:
                base = (frame * 3 + row - ROWS) * COLS
                line = far[base : base + COLS]
            else:
                line = (latent[frame, row] if frame < 4 else cache[frame - 4, row]).astype(F32)
            at = (frame * 6 + row - 1) * 3
            before = side[0, at : at + 3]
            after = side[1, at : at + 3]
            if hide:
                line, before, after = (jnp.where(last, 0.0, v) for v in (line, before, after))
            base = slot * WIDE
            raw[f, base : base + 3] = before
            raw[f, base + 3 : base + 3 + COLS] = line
            raw[f, base + 3 + COLS : base + WIDE] = after
        raw[f, 8 * WIDE : 216] = jnp.zeros((8, CM), F32)
        for lo in range(0, 216, 72):
            part = raw[f, lo : lo + 72]
            act[f, lo : lo + 72] = part if lead else normed(part, g[...], CM)
        for p in range(3):
            for q in range(3):
                top = p * WIDE + q
                low = top + 4 * WIDE
                both = jnp.concatenate([act[f, top : top + HALF], act[f, low : low + HALF]], axis=0)
                stores[f][:, (p * 3 + q) * CM : (p * 3 + q + 1) * CM] = both.astype(BF16)
    total = conv_frames(stores, w) + b[...]
    cols = lax.broadcasted_iota(jnp.int32, (PITCH, 1), 0) + (info[2] * COLS - 2)
    inside = (cols >= 0) & (cols < GRID_COLS)
    act[0, 0 : 2 * HALF] = total[: 2 * HALF]
    act[1, 0 : 2 * HALF] = total[2 * HALF :]
    for t in range(2):
        for r in range(4):
            src = (r // 2) * HALF + (r % 2) * WIDE
            res = ((r // 2) * 4 + r % 2 + 1) * WIDE + 1
            value = act[t, src : src + PITCH] + raw[2 + t, res : res + PITCH]
            out[t, r] = jnp.where(inside, value, 0.0).astype(BF16)


def first_early(info, latent, cache, below, left, right, w, b, g, out, kept, *scratch):
    @pl.when(info[0] == 0)
    def _():
        first_section(0, info, latent, cache, below, left, right, w, b, g, out, kept, *scratch)


def first_late(info, latent, below, left, right, kept, w, b, g, w_up_hbm, out, folded, *scratch):
    *scratch, w_up, sems = scratch

    @pl.when(info[0] == 0)
    def _():
        first_section(1, info, latent, None, below, left, right, w, b, g, out, kept, *scratch)

    @pl.when(info[0] == 1)
    def _():
        fold_weights(w_up_hbm, w_up, sems.at[0], folded)


def second_section(info, caches, tiles, w, b, g, out, kept, raw, act, side, far, patches):
    stores = [patches.at[0], patches.at[1], kept.at[0], kept.at[1]]
    if caches is None:
        stores = stores[2:] + stores[:2]
    first, last = info[1] == 0, info[1] == N_HA - 1
    if caches is not None:
        cache, below, above, left, right = caches
        side[0, 0:48] = left[...].astype(F32)
        side[1, 0:48] = right[...].astype(F32)
        far[0] = below[...].astype(F32)
        far[1, 0:128] = above[...].astype(F32)
    for f in range(0 if caches is not None else 2, 4):
        lead = caches is not None and f < 2
        t = f % 2
        for u in range(8):
            base = u * PITCH
            hide = first if u < 2 else (last if u > 5 else None)
            if lead:
                if 2 <= u < 6:
                    line = cache[t, u - 2].astype(F32)
                else:
                    k, at = (1, (t * 2 + u) * COLS) if u < 2 else (0, ((4 + t) * 3 + u - 6) * COLS)
                    line = far[k, at : at + COLS]
                at = (t * 8 + u) * 2
                before = side[0, at : at + 2]
                after = side[1, at : at + 2]
                if hide is not None:
                    line, before, after = (jnp.where(hide, 0.0, v) for v in (line, before, after))
                raw[f, base : base + 2] = before
                raw[f, base + 2 : base + 22] = line
                raw[f, base + 22 : base + 24] = after
            else:
                low, top = tiles
                line = (top[t, u] if u < 4 else low[t, u - 4]).astype(F32)
                raw[f, base : base + PITCH] = line if hide is None else jnp.where(hide, 0.0, line)
        raw[f, 8 * PITCH : 200] = jnp.zeros((8, CM), F32)
        for lo, hi in ((0, 96), (96, 200)):
            part = raw[f, lo:hi]
            act[f, lo:hi] = part if lead else normed(part, g[...], CM)
        for p in range(3):
            for q in range(3):
                at = p * PITCH + q
                stores[f][:, (p * 3 + q) * CM : (p * 3 + q + 1) * CM] = act[f, at : at + 144].astype(BF16)
    total = conv_frames(stores, w) + b[...]
    cell = lax.broadcasted_iota(jnp.int32, (PITCH, 1), 0)
    cols = cell + (info[2] * COLS - 1)
    inside = (cols >= 0) & (cols < GRID_COLS) & (cell < 22)
    for t in range(2):
        for i in range(6):
            row_at = info[1] * ROWS - 1 + i
            fits = inside & (row_at >= 0) & (row_at < GRID_ROWS)
            res = (i + 1) * PITCH + 1
            at = t * 144 + i * PITCH
            value = total[at : at + PITCH] + raw[2 + t, res : res + PITCH]
            out[at : at + PITCH] = jnp.where(fits, value, 0.0).astype(BF16)


def second_early(info, cache, below, above, left, right, low, top, w, b, g, w_up_hbm, out, kept, folded, *scratch):
    *scratch, ring, w_up, sems = scratch

    @pl.when(info[0] == 1)
    def _():
        second_section(info, (cache, below, above, left, right), (low, top), w, b, g, out, kept, *scratch)
        first, last = info[1] == 0, info[1] == N_HA - 1
        side, far = scratch[2:4]
        ring[...] = jnp.zeros((112, CM), F32)
        for at, e, line, hide in ((0, 0, far[1, 80:120], first), (48, 9, far[0, 0:40], last)):
            ring[at : at + 1] = jnp.where(hide, 0.0, side[0, 32 + e : 33 + e])
            ring[at + 1 : at + 41] = jnp.where(hide, 0.0, line)
            ring[at + 41 : at + 42] = jnp.where(hide, 0.0, side[1, 32 + e : 33 + e])
        ring[96:104] = side[0, 33:41]
        ring[104:112] = side[1, 33:41]
        out[RING : RING + 112] = ring[...].astype(BF16)

    @pl.when(info[0] == 0)
    def _():
        fold_weights(w_up_hbm, w_up, sems.at[0], folded)


def second_late(info, low, top, kept, w, b, g, out, *scratch):
    @pl.when(info[0] == 1)
    def _():
        second_section(info, None, (low, top), w, b, g, out, kept, *scratch)


def last_section(info, lead, main, returned, cache, folded_0, folded_1, b_up, g, w_hbm, b,
                 out, coarse, ups, act, rows, ring, patches, wide, w, sems):
    copy = pltpu.make_async_copy(w_hbm, w.at[:, pl.ds(0, CF)], sems.at[0])
    copy.start()
    for k in range(27):
        w[k, CF:256] = jnp.zeros((64, CF), BF16)
    lanes = lambda ref: jnp.concatenate([ref[...], jnp.zeros((1, 64), F32)], axis=1)
    bias, gain = lanes(b_up), lanes(g)

    def upsample(src, w_up, slot, keep):
        for t in range(2):
            coarse[t, 0:144] = src[t * 144 : t * 144 + 144].astype(F32)
            coarse[t, 144:160] = jnp.zeros((16, CM), F32)
        lhs = [
            jnp.concatenate([coarse[t, du * PITCH + dv : du * PITCH + dv + 128].astype(BF16) for t in range(2)], axis=0)
            for du in range(2)
            for dv in range(2)
        ]
        lhs = jnp.concatenate(lhs, axis=1)
        cell = lax.broadcasted_iota(jnp.int32, (128, 1), 0)
        col = lax.rem(cell, PITCH)
        for phase in range(4):
            br, bc = phase // 2, phase % 2
            total = jnp.dot(lhs, w_up[:, phase * 256 : phase * 256 + 256], preferred_element_type=F32)
            value = (total + bias).astype(BF16).astype(F32)
            if br == 0:
                outside = (cell < PITCH) & (info[1] == 0)
            else:
                outside = (cell >= 4 * PITCH) & (info[1] == N_HA - 1)
            if bc == 0:
                outside |= (col == 0) & (info[2] == 0)
            else:
                outside |= (col == COLS) & (info[2] == N_WA - 1)
            unit = normed(value, gain, CF)
            for t in range(2):
                if keep:
                    ups[t, phase] = value[t * 128 : t * 128 + 128]
                act[slot + t, phase] = jnp.where(outside, 0.0, unit[t * 128 : t * 128 + 128])

    @pl.when(info[0] == 0)
    def _():
        rows[...] = jnp.zeros((2, 56, 128), F32)
        ring[...] = returned[RING : RING + 112].astype(F32)
        for t in range(2):
            part = slice(t * CF, t * CF + CF)
            for e in range(10):
                if e == 0 or e == 9:
                    at = 0 if e == 0 else 48
                    line = ring[at : at + 48][:, part]
                    rows[0, 0:48] = line[:, :128]
                    rows[1, 0:48, 0:64] = line[:, 128:]
                else:
                    line = cache[t, e - 1].astype(F32)
                    rows[0, 1:41] = line[:, :128]
                    rows[1, 1:41, 0:64] = line[:, 128:]
                    for at, col in ((95 + e, 0), (103 + e, 41)):
                        end = ring[at : at + 1][:, part]
                        rows[0, col : col + 1] = end[:, :128]
                        rows[1, col : col + 1, 0:64] = end[:, 128:]
                br, u = e % 2, e // 2
                for bc in range(2):
                    for c in range(2):
                        act[t, br * 2 + bc, u * PITCH : (u + 1) * PITCH, c * 128 : c * 128 + 128] = rows[
                            c, pl.ds(bc, PITCH, 2), :
                        ]
        upsample(returned, folded_0, 2, True)

    @pl.when(info[0] == 1)
    def _():
        upsample(lead, folded_1, 0, False)
        upsample(main, folded_1, 2, True)

    for f in range(4):
        for plane in range(4):
            for s in range(4):
                at = (s // 2) * PITCH + s % 2
                patches[f, plane * 4 + s] = act[f, plane, at : at + 96].astype(BF16)
    copy.wait()
    for yb in range(2):
        for xb in range(2):
            total = None
            blocks = [
                (((yb + p) % 2) * 2 + (xb + q) % 2) * 4 + ((yb + p) // 2) * 2 + (xb + q) // 2
                for p in range(3)
                for q in range(3)
            ]
            for a in range(3):
                lhs = jnp.concatenate([patches[a : a + 2, block].reshape(192, 256) for block in blocks], axis=1)
                taps = w[a * 9 : a * 9 + 9].reshape(9 * 256, CF)
                part = jnp.dot(lhs, taps, preferred_element_type=F32)
                total = part if total is None else total + part
            total = total + b[...]
            plane = ((yb + 1) % 2) * 2 + (xb + 1) % 2
            at = ((yb + 1) // 2) * PITCH + (xb + 1) // 2
            for t in range(2):
                value = total[t * 96 : t * 96 + 96] + ups[t, plane, at : at + 96][:, :CF]
                for y in range(4):
                    line = value[y * PITCH : y * PITCH + COLS]
                    wide[0, t, 2 * y + yb, pl.ds(xb, COLS, 2), :] = line[:, :128]
                    wide[1, t, 2 * y + yb, pl.ds(xb, COLS, 2), :] = jnp.concatenate(
                        [line[:, 128:], line[:, 128:]], axis=1
                    )
    for t in range(2):
        for y in range(8):
            out[t, y, :, :128] = wide[0, t, y].astype(BF16)
            out[t, y, :, 128:] = wide[1, t, y][:, :64].astype(BF16)


VMEM = pl.BlockSpec(memory_space=pltpu.VMEM)
SMEM = pl.BlockSpec(memory_space=pltpu.SMEM)
HBM = pl.BlockSpec(memory_space=pltpu.HBM)


def call(body, specs, outs, scratch, *operands, flops=0, megabytes=20):
    kinds = {"s": SMEM, "v": VMEM, "h": HBM}
    return pl.pallas_call(
        body,
        out_shape=[jax.ShapeDtypeStruct(shape, BF16) for shape in outs],
        in_specs=[kinds[c] for c in specs],
        out_specs=[VMEM] * len(outs),
        scratch_shapes=scratch,
        compiler_params=pltpu.CompilerParams(vmem_limit_bytes=megabytes * 2**20),
        cost_estimate=pl.CostEstimate(flops=flops, bytes_accessed=2**20, transcendentals=0),
    )(*operands)


def device_at(s, h, w):
    return (s * N_HA + h) * N_WA + w


def pairs_between(src_seg, dst_seg, dh, dw, wrap=False):
    pairs = []
    for h in range(N_HA):
        for w in range(N_WA):
            if (wrap or 0 <= h - dh < N_HA) and 0 <= w - dw < N_WA:
                pairs.append((device_at(src_seg, (h - dh) % N_HA, w - dw), device_at(dst_seg, h, w)))
    return pairs


def shards(latent, w_mid, b_mid, g_mid, cache_mid, w_up, b_up, g_fine, cache_fine, w_fine, b_fine):
    info = jnp.stack([lax.axis_index(axis) for axis in AXES]).astype(jnp.int32)
    kernel = w_mid.reshape(3, 9 * CM, CM)
    up_kernel = jnp.swapaxes(w_up, 2, 3).reshape(9, CF, CM)
    dma = pltpu.SemaphoreType.DMA

    cache = cache_mid[0]
    side = pltpu.VMEM((2, 112, CM), F32)
    far = lambda count: pltpu.VMEM((count, 368, CM) if count > 1 else (368, CM), F32)
    to_above, to_below = call(
        pack_rows, "svvv", [(368, CM), (128, CM)], [far(1)], info, latent, cache, cache_fine, megabytes=3
    )
    below = lax.ppermute(to_above, "ha", [(i, (i - 1) % N_HA) for i in range(N_HA)])
    above = lax.ppermute(to_below, AXES, pairs_between(1, 1, 1, 0))
    sides = call(
        pack_columns, "svvvvv", [(112, CM)] * 2 + [(48, CM)] * 2, [far(2), side],
        info, latent, cache, cache_fine, below, above, megabytes=3, flops=2 * 10**9,
    )
    right_0, left_0 = (lax.ppermute(sides[k], AXES, pairs_between(0, 0, 0, 2 * k - 1)) for k in range(2))
    right_1, left_1 = (lax.ppermute(sides[2 + k], AXES, pairs_between(1, 1, 0, 2 * k - 1)) for k in range(2))

    up_scratch = [pltpu.VMEM((9, CF, CM), BF16), dma((1,))]
    folded_shape = (4 * CM, 1024)
    first_scratch = [
        pltpu.VMEM((4, 216, CM), F32),
        pltpu.VMEM((4, 216, CM), F32),
        side,
        far(1),
        pltpu.VMEM((2, 2 * HALF, 9 * CM), BF16),
    ]
    first_shape = (2, ROWS, PITCH, CM)
    first_flops = 2 * 224 * 27 * CM * CM
    spread = lambda tile: [lax.ppermute(tile, AXES, pairs_between(0, 1, dh, 0, True)) for dh in range(2)]
    early, kept = call(
        first_early, "svvvvvvvv", [first_shape, (2, 2 * HALF, 9 * CM)], first_scratch,
        info, latent, cache, below, left_0, right_0, kernel, b_mid, g_mid, flops=first_flops, megabytes=16,
    )
    group_a = spread(early)
    late, folded_1 = call(
        first_late, "svvvvvvvvh", [first_shape, folded_shape], first_scratch + up_scratch,
        info, latent, below, left_0, right_0, kept, kernel, b_mid, g_mid, up_kernel, flops=first_flops, megabytes=16,
    )
    group_b = spread(late)

    second_scratch = [
        pltpu.VMEM((4, 200, CM), F32),
        pltpu.VMEM((4, 200, CM), F32),
        side,
        far(2),
        pltpu.VMEM((2, 144, 9 * CM), BF16),
    ]
    second_flops = 2 * 288 * 27 * CM * CM
    second_a, kept, folded_0 = call(
        second_early, "svvvvvvvvvvh", [(RING + 112, CM), (2, 144, 9 * CM), folded_shape],
        second_scratch + [pltpu.VMEM((112, CM), F32)] + up_scratch,
        info, cache, below, above, left_1, right_1, *group_a, kernel, b_mid, g_mid, up_kernel, flops=second_flops, megabytes=16,
    )
    returned = lax.ppermute(second_a, "segment", [(1, 0)])
    (second_b,) = call(
        second_late, "svvvvvv", [(RING, CM)], second_scratch,
        info, *group_b, kept, kernel, b_mid, g_mid, flops=second_flops, megabytes=16,
    )
    (decoded,) = call(
        last_section, "svvvvvvvvhv", [(2, 8, 40, CF)],
        [
            pltpu.VMEM((2, 160, CM), F32),
            pltpu.VMEM((2, 4, 128, 256), F32),
            pltpu.VMEM((4, 4, 128, 256), F32),
            pltpu.VMEM((2, 56, 128), F32),
            pltpu.VMEM((112, CM), F32),
            pltpu.VMEM((4, 16, 96, 256), BF16),
            pltpu.VMEM((2, 2, 8, 40, 128), F32),
            pltpu.VMEM((27, 256, CF), BF16),
            dma((1,)),
        ],
        info, second_a, second_b, returned, cache_fine, folded_0, folded_1,
        b_up[None], g_fine[None], w_fine.reshape(27, CF, CF), b_fine[None],
        flops=2 * 768 * 27 * CF * CF, megabytes=16,
    )
    return decoded


def solution(mesh):
    return jax.shard_map(
        shards,
        mesh=mesh,
        in_specs=(
            P(None, "ha", "wa", None),
            P("segment", None, None, None, None, None),
            P("segment", None),
            P("segment", None),
            P("segment", None, "ha", "wa", None),
            P(),
            P(),
            P(),
            P(None, "ha", "wa", None),
            P(),
            P(),
        ),
        out_specs=P("segment", "ha", "wa", None),
        check_vma=False,
    )
```

```python
import jax
import jax.numpy as jnp
from jax import lax
from jax.experimental import pallas as pl
from jax.experimental.pallas import tpu as pltpu
from jax.sharding import PartitionSpec as P

F32 = jnp.float32
BF16 = jnp.bfloat16
CM = 384
CF = 192
AXES = ("segment", "ha", "wa")
N_HA = 8
N_WA = 16
GRID_ROWS = 32
GRID_COLS = 320
ROWS = 4
COLS = 20
PITCH = 24
WIDE = 26
HALF = 56
RING = 2 * 6 * PITCH


def normed(values, gain_vec, channels):
    inv_rms = lax.rsqrt(jnp.sum(values * values, axis=-1, keepdims=True) * (1.0 / channels) + 1e-06)
    scaled = values * inv_rms * gain_vec
    half = 0.5 * scaled
    return half + half * jnp.tanh(half)


def conv_frames(stores, w):
    total = None
    for a in range(3):
        lhs = jnp.concatenate([stores[a][...], stores[a + 1][...]], axis=0)
        part = jnp.dot(lhs, w[a], preferred_element_type=F32)
        total = part if total is None else total + part
    return total


def frame_pair(first, second):
    return jnp.concatenate([first.astype(F32), second.astype(F32)], axis=1)


def pack_rows(info, latent, cache, to_above, side):
    for f in range(2):
        for row in range(3):
            at = ((4 + f) * 3 + row) * COLS
            side[at : at + COLS] = cache[f, row].astype(F32)

    @pl.when(info[0] == 0)
    def _():
        for f in range(4):
            for row in range(3):
                at = (f * 3 + row) * COLS
                side[at : at + COLS] = latent[f, row].astype(F32)

    to_above[...] = side[...].astype(BF16)


def pack_caches(info, cache, fine, _, to_below, fine_up, side):
    @pl.when(info[0] == 1)
    def _():
        for f in range(2):
            for row in range(2):
                at = (f * 2 + row) * COLS
                side[at : at + COLS] = cache[f, 2 + row].astype(F32)
        side[80:120] = frame_pair(fine[0, 7], fine[1, 7])
        to_below[...] = side[...].astype(BF16)
        side[0:40] = frame_pair(fine[0, 0], fine[1, 0])
        fine_up[...] = side[0:48].astype(BF16)


def pack_columns(info, latent, cache, fine, below, above, under, left_0, right_0, left_1, right_1, far, side):
    far[0] = below[...].astype(F32)

    @pl.when(info[0] == 0)
    def _():
        for f in range(6):
            for row in range(1, 7):
                if row < ROWS:
                    line = (latent[f, row] if f < 4 else cache[f - 4, row]).astype(F32)
                    first, final = line[:3], line[17:20]
                else:
                    base = (f * 3 + row - ROWS) * COLS
                    first, final = far[0, base : base + 3], far[0, base + 17 : base + 20]
                at = (f * 6 + row - 1) * 3
                side[0, at : at + 3] = first
                side[1, at : at + 3] = final
        left_0[...] = side[0].astype(BF16)
        right_0[...] = side[1].astype(BF16)

    @pl.when(info[0] == 1)
    def _():
        far[1, 0:128] = above[...].astype(F32)
        far[1, 128:176] = under[...].astype(F32)
        for t in range(2):
            for u in range(8):
                if 2 <= u < 6:
                    line = cache[t, u - 2].astype(F32)
                    first, final = line[:2], line[18:20]
                else:
                    k, base = (1, (t * 2 + u) * COLS) if u < 2 else (0, ((4 + t) * 3 + u - 6) * COLS)
                    first, final = far[k, base : base + 2], far[k, base + 18 : base + 20]
                at = (t * 8 + u) * 2
                side[0, at : at + 2] = first
                side[1, at : at + 2] = final
        for e in range(10):
            if 1 <= e <= 8:
                line = frame_pair(fine[0, e - 1], fine[1, e - 1])
                first, final = line[0:1], line[39:40]
            else:
                k, base = (1, 80) if e == 0 else (1, 128)
                first, final = far[k, base : base + 1], far[k, base + 39 : base + 40]
            side[0, 32 + e : 33 + e] = first
            side[1, 32 + e : 33 + e] = final
        left_1[...] = side[0, 0:48].astype(BF16)
        right_1[...] = side[1, 0:48].astype(BF16)


def fold_weights(w_up_hbm, w_up, sem, out):
    copy = pltpu.make_async_copy(w_up_hbm, w_up, sem)
    copy.start()
    copy.wait()
    zeros = jnp.zeros((CM, 64), F32)
    taps = [jnp.transpose(w_up[k].astype(F32)) for k in range(9)]
    for br in range(2):
        for bc in range(2):
            place = br * 2 + bc
            for du in range(2):
                ps = ((0, 1), (2,))[du] if br == 0 else ((0,), (1, 2))[du]
                for dv in range(2):
                    qs = ((0, 1), (2,))[dv] if bc == 0 else ((0,), (1, 2))[dv]
                    total = None
                    for p in ps:
                        for q in qs:
                            part = taps[p * 3 + q]
                            total = part if total is None else total + part
                    both = jnp.concatenate([total, zeros], axis=1).astype(BF16)
                    out[(du * 2 + dv) * CM : (du * 2 + dv + 1) * CM, place * 256 : place * 256 + 256] = both


def first_section(group, info, latent, cache, below, left, right, w, b, g, out, kept, raw, act, side, far, patches):
    stores = [patches.at[0], patches.at[1], kept.at[0], kept.at[1]]
    if group == 1:
        stores = stores[2:] + stores[:2]
    last = info[1] == N_HA - 1
    side[0] = left[...].astype(F32)
    side[1] = right[...].astype(F32)
    far[...] = below[...].astype(F32)
    slots = [(1, False), (2, False), (3, False), (4, True), (3, True), (4, False), (5, False), (6, False)]
    for f in range(2 * group, 4):
        lead = group == 0 and f < 2
        frame = f if group == 1 else (4 + f if lead else f - 2)
        for slot, (row, hide) in enumerate(slots):
            if row >= ROWS:
                base = (frame * 3 + row - ROWS) * COLS
                line = far[base : base + COLS]
            else:
                line = (latent[frame, row] if frame < 4 else cache[frame - 4, row]).astype(F32)
            at = (frame * 6 + row - 1) * 3
            before = side[0, at : at + 3]
            after = side[1, at : at + 3]
            if hide:
                line, before, after = (jnp.where(last, 0.0, v) for v in (line, before, after))
            base = slot * WIDE
            raw[f, base : base + 3] = before
            raw[f, base + 3 : base + 3 + COLS] = line
            raw[f, base + 3 + COLS : base + WIDE] = after
        raw[f, 8 * WIDE : 216] = jnp.zeros((8, CM), F32)
        for lo in range(0, 216, 72):
            part = raw[f, lo : lo + 72]
            act[f, lo : lo + 72] = part if lead else normed(part, g[...], CM)
        for p in range(3):
            for q in range(3):
                top = p * WIDE + q
                low = top + 4 * WIDE
                both = jnp.concatenate([act[f, top : top + HALF], act[f, low : low + HALF]], axis=0)
                stores[f][:, (p * 3 + q) * CM : (p * 3 + q + 1) * CM] = both.astype(BF16)
    total = conv_frames(stores, w) + b[...]
    cols = lax.broadcasted_iota(jnp.int32, (PITCH, 1), 0) + (info[2] * COLS - 2)
    inside = (cols >= 0) & (cols < GRID_COLS)
    act[0, 0 : 2 * HALF] = total[: 2 * HALF]
    act[1, 0 : 2 * HALF] = total[2 * HALF :]
    for t in range(2):
        for r in range(4):
            src = (r // 2) * HALF + (r % 2) * WIDE
            res = ((r // 2) * 4 + r % 2 + 1) * WIDE + 1
            value = act[t, src : src + PITCH] + raw[2 + t, res : res + PITCH]
            out[t, r] = jnp.where(inside, value, 0.0).astype(BF16)


def first_early(info, latent, cache, below, left, right, w, b, g, out, kept, *scratch):
    @pl.when(info[0] == 0)
    def _():
        first_section(0, info, latent, cache, below, left, right, w, b, g, out, kept, *scratch)


def first_late(info, latent, below, left, right, kept, w, b, g, w_up_hbm, out, folded, *scratch):
    *scratch, w_up, sems = scratch

    @pl.when(info[0] == 0)
    def _():
        first_section(1, info, latent, None, below, left, right, w, b, g, out, kept, *scratch)

    @pl.when(info[0] == 1)
    def _():
        fold_weights(w_up_hbm, w_up, sems.at[0], folded)


def second_section(info, caches, tiles, w, b, g, out, kept, raw, act, side, far, patches):
    stores = [patches.at[0], patches.at[1], kept.at[0], kept.at[1]]
    if caches is None:
        stores = stores[2:] + stores[:2]
    first, last = info[1] == 0, info[1] == N_HA - 1
    if caches is not None:
        cache, below, above, under, left, right = caches
        far[1, 128:176] = under[...].astype(F32)
        side[0, 0:48] = left[...].astype(F32)
        side[1, 0:48] = right[...].astype(F32)
        far[0] = below[...].astype(F32)
        far[1, 0:128] = above[...].astype(F32)
    for f in range(0 if caches is not None else 2, 4):
        lead = caches is not None and f < 2
        t = f % 2
        for u in range(8):
            base = u * PITCH
            hide = first if u < 2 else (last if u > 5 else None)
            if lead:
                if 2 <= u < 6:
                    line = cache[t, u - 2].astype(F32)
                else:
                    k, at = (1, (t * 2 + u) * COLS) if u < 2 else (0, ((4 + t) * 3 + u - 6) * COLS)
                    line = far[k, at : at + COLS]
                at = (t * 8 + u) * 2
                before = side[0, at : at + 2]
                after = side[1, at : at + 2]
                if hide is not None:
                    line, before, after = (jnp.where(hide, 0.0, v) for v in (line, before, after))
                raw[f, base : base + 2] = before
                raw[f, base + 2 : base + 22] = line
                raw[f, base + 22 : base + 24] = after
            else:
                low, top = tiles
                line = (top[t, u] if u < 4 else low[t, u - 4]).astype(F32)
                raw[f, base : base + PITCH] = line if hide is None else jnp.where(hide, 0.0, line)
        raw[f, 8 * PITCH : 200] = jnp.zeros((8, CM), F32)
        for lo, hi in ((0, 96), (96, 200)):
            part = raw[f, lo:hi]
            act[f, lo:hi] = part if lead else normed(part, g[...], CM)
        for p in range(3):
            for q in range(3):
                at = p * PITCH + q
                stores[f][:, (p * 3 + q) * CM : (p * 3 + q + 1) * CM] = act[f, at : at + 144].astype(BF16)
    total = conv_frames(stores, w) + b[...]
    cell = lax.broadcasted_iota(jnp.int32, (PITCH, 1), 0)
    cols = cell + (info[2] * COLS - 1)
    inside = (cols >= 0) & (cols < GRID_COLS) & (cell < 22)
    for t in range(2):
        for i in range(6):
            row_at = info[1] * ROWS - 1 + i
            fits = inside & (row_at >= 0) & (row_at < GRID_ROWS)
            res = (i + 1) * PITCH + 1
            at = t * 144 + i * PITCH
            value = total[at : at + PITCH] + raw[2 + t, res : res + PITCH]
            out[at : at + PITCH] = jnp.where(fits, value, 0.0).astype(BF16)


def second_early(info, cache, below, above, under, left, right, low, top, w, b, g, w_up_hbm, out, kept, folded, *scratch):
    *scratch, ring, w_up, sems = scratch

    @pl.when(info[0] == 1)
    def _():
        second_section(info, (cache, below, above, under, left, right), (low, top), w, b, g, out, kept, *scratch)
        first, last = info[1] == 0, info[1] == N_HA - 1
        side, far = scratch[2:4]
        ring[...] = jnp.zeros((112, CM), F32)
        for at, e, line, hide in ((0, 0, far[1, 80:120], first), (48, 9, far[1, 128:168], last)):
            ring[at : at + 1] = jnp.where(hide, 0.0, side[0, 32 + e : 33 + e])
            ring[at + 1 : at + 41] = jnp.where(hide, 0.0, line)
            ring[at + 41 : at + 42] = jnp.where(hide, 0.0, side[1, 32 + e : 33 + e])
        ring[96:104] = side[0, 33:41]
        ring[104:112] = side[1, 33:41]
        out[RING : RING + 112] = ring[...].astype(BF16)

    @pl.when(info[0] == 0)
    def _():
        fold_weights(w_up_hbm, w_up, sems.at[0], folded)


def second_late(info, low, top, kept, w, b, g, out, *scratch):
    @pl.when(info[0] == 1)
    def _():
        second_section(info, None, (low, top), w, b, g, out, kept, *scratch)


def last_section(info, lead, main, returned, cache, folded_0, folded_1, b_up, g, w_hbm, b,
                 out, coarse, ups, act, rows, ring, patches, wide, w, sems):
    copy = pltpu.make_async_copy(w_hbm, w.at[:, pl.ds(0, CF)], sems.at[0])
    copy.start()
    for k in range(27):
        w[k, CF:256] = jnp.zeros((64, CF), BF16)
    lanes = lambda ref: jnp.concatenate([ref[...], jnp.zeros((1, 64), F32)], axis=1)
    bias, gain = lanes(b_up), lanes(g)

    def upsample(src, w_up, slot, keep):
        for t in range(2):
            coarse[t, 0:144] = src[t * 144 : t * 144 + 144].astype(F32)
            coarse[t, 144:160] = jnp.zeros((16, CM), F32)
        lhs = [
            jnp.concatenate([coarse[t, du * PITCH + dv : du * PITCH + dv + 128].astype(BF16) for t in range(2)], axis=0)
            for du in range(2)
            for dv in range(2)
        ]
        lhs = jnp.concatenate(lhs, axis=1)
        cell = lax.broadcasted_iota(jnp.int32, (128, 1), 0)
        col = lax.rem(cell, PITCH)
        for phase in range(4):
            br, bc = phase // 2, phase % 2
            total = jnp.dot(lhs, w_up[:, phase * 256 : phase * 256 + 256], preferred_element_type=F32)
            value = (total + bias).astype(BF16).astype(F32)
            if br == 0:
                outside = (cell < PITCH) & (info[1] == 0)
            else:
                outside = (cell >= 4 * PITCH) & (info[1] == N_HA - 1)
            if bc == 0:
                outside |= (col == 0) & (info[2] == 0)
            else:
                outside |= (col == COLS) & (info[2] == N_WA - 1)
            unit = normed(value, gain, CF)
            for t in range(2):
                if keep:
                    ups[t, phase] = value[t * 128 : t * 128 + 128]
                act[slot + t, phase] = jnp.where(outside, 0.0, unit[t * 128 : t * 128 + 128])

    @pl.when(info[0] == 0)
    def _():
        rows[...] = jnp.zeros((2, 56, 128), F32)
        ring[...] = returned[RING : RING + 112].astype(F32)
        for t in range(2):
            part = slice(t * CF, t * CF + CF)
            for e in range(10):
                if e == 0 or e == 9:
                    at = 0 if e == 0 else 48
                    line = ring[at : at + 48][:, part]
                    rows[0, 0:48] = line[:, :128]
                    rows[1, 0:48, 0:64] = line[:, 128:]
                else:
                    line = cache[t, e - 1].astype(F32)
                    rows[0, 1:41] = line[:, :128]
                    rows[1, 1:41, 0:64] = line[:, 128:]
                    for at, col in ((95 + e, 0), (103 + e, 41)):
                        end = ring[at : at + 1][:, part]
                        rows[0, col : col + 1] = end[:, :128]
                        rows[1, col : col + 1, 0:64] = end[:, 128:]
                br, u = e % 2, e // 2
                for bc in range(2):
                    for c in range(2):
                        act[t, br * 2 + bc, u * PITCH : (u + 1) * PITCH, c * 128 : c * 128 + 128] = rows[
                            c, pl.ds(bc, PITCH, 2), :
                        ]
        upsample(returned, folded_0, 2, True)

    @pl.when(info[0] == 1)
    def _():
        upsample(lead, folded_1, 0, False)
        upsample(main, folded_1, 2, True)

    for f in range(4):
        for plane in range(4):
            for s in range(4):
                at = (s // 2) * PITCH + s % 2
                patches[f, plane * 4 + s] = act[f, plane, at : at + 96].astype(BF16)
    copy.wait()
    for yb in range(2):
        for xb in range(2):
            total = None
            blocks = [
                (((yb + p) % 2) * 2 + (xb + q) % 2) * 4 + ((yb + p) // 2) * 2 + (xb + q) // 2
                for p in range(3)
                for q in range(3)
            ]
            for a in range(3):
                lhs = jnp.concatenate([patches[a : a + 2, block].reshape(192, 256) for block in blocks], axis=1)
                taps = w[a * 9 : a * 9 + 9].reshape(9 * 256, CF)
                part = jnp.dot(lhs, taps, preferred_element_type=F32)
                total = part if total is None else total + part
            total = total + b[...]
            plane = ((yb + 1) % 2) * 2 + (xb + 1) % 2
            at = ((yb + 1) // 2) * PITCH + (xb + 1) // 2
            for t in range(2):
                value = total[t * 96 : t * 96 + 96] + ups[t, plane, at : at + 96][:, :CF]
                for y in range(4):
                    line = value[y * PITCH : y * PITCH + COLS]
                    wide[0, t, 2 * y + yb, pl.ds(xb, COLS, 2), :] = line[:, :128]
                    wide[1, t, 2 * y + yb, pl.ds(xb, COLS, 2), :] = jnp.concatenate(
                        [line[:, 128:], line[:, 128:]], axis=1
                    )
    for t in range(2):
        for y in range(8):
            out[t, y, :, :128] = wide[0, t, y].astype(BF16)
            out[t, y, :, 128:] = wide[1, t, y][:, :64].astype(BF16)


VMEM = pl.BlockSpec(memory_space=pltpu.VMEM)
SMEM = pl.BlockSpec(memory_space=pltpu.SMEM)
HBM = pl.BlockSpec(memory_space=pltpu.HBM)


def call(body, specs, outs, scratch, *operands, flops=0, megabytes=20):
    kinds = {"s": SMEM, "v": VMEM, "h": HBM}
    return pl.pallas_call(
        body,
        out_shape=[jax.ShapeDtypeStruct(shape, BF16) for shape in outs],
        in_specs=[kinds[c] for c in specs],
        out_specs=[VMEM] * len(outs),
        scratch_shapes=scratch,
        compiler_params=pltpu.CompilerParams(vmem_limit_bytes=megabytes * 2**20),
        cost_estimate=pl.CostEstimate(flops=flops, bytes_accessed=2**20, transcendentals=0),
    )(*operands)


def device_at(s, h, w):
    return (s * N_HA + h) * N_WA + w


def pairs_between(src_seg, dst_seg, dh, dw, wrap=False):
    pairs = []
    for h in range(N_HA):
        for w in range(N_WA):
            if (wrap or 0 <= h - dh < N_HA) and 0 <= w - dw < N_WA:
                pairs.append((device_at(src_seg, (h - dh) % N_HA, w - dw), device_at(dst_seg, h, w)))
    return pairs


def shards(latent, w_mid, b_mid, g_mid, cache_mid, w_up, b_up, g_fine, cache_fine, w_fine, b_fine):
    info = jnp.stack([lax.axis_index(axis) for axis in AXES]).astype(jnp.int32)
    kernel = w_mid.reshape(3, 9 * CM, CM)
    up_kernel = jnp.swapaxes(w_up, 2, 3).reshape(9, CF, CM)
    dma = pltpu.SemaphoreType.DMA

    cache = cache_mid[0]
    side = pltpu.VMEM((2, 112, CM), F32)
    far = lambda count: pltpu.VMEM((count, 368, CM) if count > 1 else (368, CM), F32)
    (to_above,) = call(pack_rows, "svv", [(368, CM)], [far(1)], info, latent, cache, megabytes=3)
    below = lax.ppermute(to_above, "ha", [(i, (i - 1) % N_HA) for i in range(N_HA)])
    to_below, fine_up = call(
        pack_caches, "svvv", [(128, CM), (48, CM)], [pltpu.VMEM((128, CM), F32)], info, cache, cache_fine, to_above,
        megabytes=3,
    )
    above = lax.ppermute(to_below, AXES, pairs_between(1, 1, 1, 0))
    under = lax.ppermute(fine_up, AXES, pairs_between(1, 1, -1, 0))
    sides = call(
        pack_columns, "svvvvvv", [(112, CM)] * 2 + [(48, CM)] * 2, [far(2), side],
        info, latent, cache, cache_fine, below, above, under, megabytes=3, flops=2 * 10**9,
    )
    right_0, left_0 = (lax.ppermute(sides[k], AXES, pairs_between(0, 0, 0, 2 * k - 1)) for k in range(2))
    right_1, left_1 = (lax.ppermute(sides[2 + k], AXES, pairs_between(1, 1, 0, 2 * k - 1)) for k in range(2))

    up_scratch = [pltpu.VMEM((9, CF, CM), BF16), dma((1,))]
    folded_shape = (4 * CM, 1024)
    first_scratch = [
        pltpu.VMEM((4, 216, CM), F32),
        pltpu.VMEM((4, 216, CM), F32),
        side,
        far(1),
        pltpu.VMEM((2, 2 * HALF, 9 * CM), BF16),
    ]
    first_shape = (2, ROWS, PITCH, CM)
    first_flops = 2 * 224 * 27 * CM * CM
    spread = lambda tile: [lax.ppermute(tile, AXES, pairs_between(0, 1, dh, 0, True)) for dh in range(2)]
    early, kept = call(
        first_early, "svvvvvvvv", [first_shape, (2, 2 * HALF, 9 * CM)], first_scratch,
        info, latent, cache, below, left_0, right_0, kernel, b_mid, g_mid, flops=first_flops, megabytes=16,
    )
    group_a = spread(early)
    late, folded_1 = call(
        first_late, "svvvvvvvvh", [first_shape, folded_shape], first_scratch + up_scratch,
        info, latent, below, left_0, right_0, kept, kernel, b_mid, g_mid, up_kernel, flops=first_flops, megabytes=16,
    )
    group_b = spread(late)

    second_scratch = [
        pltpu.VMEM((4, 200, CM), F32),
        pltpu.VMEM((4, 200, CM), F32),
        side,
        far(2),
        pltpu.VMEM((2, 144, 9 * CM), BF16),
    ]
    second_flops = 2 * 288 * 27 * CM * CM
    second_a, kept, folded_0 = call(
        second_early, "svvvvvvvvvvvh", [(RING + 112, CM), (2, 144, 9 * CM), folded_shape],
        second_scratch + [pltpu.VMEM((112, CM), F32)] + up_scratch,
        info, cache, below, above, under, left_1, right_1, *group_a, kernel, b_mid, g_mid, up_kernel, flops=second_flops, megabytes=16,
    )
    returned = lax.ppermute(second_a, "segment", [(1, 0)])
    (second_b,) = call(
        second_late, "svvvvvv", [(RING, CM)], second_scratch,
        info, *group_b, kept, kernel, b_mid, g_mid, flops=second_flops, megabytes=16,
    )
    (decoded,) = call(
        last_section, "svvvvvvvvhv", [(2, 8, 40, CF)],
        [
            pltpu.VMEM((2, 160, CM), F32),
            pltpu.VMEM((2, 4, 128, 256), F32),
            pltpu.VMEM((4, 4, 128, 256), F32),
            pltpu.VMEM((2, 56, 128), F32),
            pltpu.VMEM((112, CM), F32),
            pltpu.VMEM((4, 16, 96, 256), BF16),
            pltpu.VMEM((2, 2, 8, 40, 128), F32),
            pltpu.VMEM((27, 256, CF), BF16),
            dma((1,)),
        ],
        info, second_a, second_b, returned, cache_fine, folded_0, folded_1,
        b_up[None], g_fine[None], w_fine.reshape(27, CF, CF), b_fine[None],
        flops=2 * 768 * 27 * CF * CF, megabytes=16,
    )
    return decoded


def solution(mesh):
    return jax.shard_map(
        shards,
        mesh=mesh,
        in_specs=(
            P(None, "ha", "wa", None),
            P("segment", None, None, None, None, None),
            P("segment", None),
            P("segment", None),
            P("segment", None, "ha", "wa", None),
            P(),
            P(),
            P(),
            P(None, "ha", "wa", None),
            P(),
            P(),
        ),
        out_specs=P("segment", "ha", "wa", None),
        check_vma=False,
    )
```

```python
import jax
import jax.numpy as jnp
from jax import lax
from jax.experimental import pallas as pl
from jax.experimental.pallas import tpu as pltpu
from jax.sharding import PartitionSpec as P

F32 = jnp.float32
BF16 = jnp.bfloat16
CM = 384
CF = 192
AXES = ("segment", "ha", "wa")
N_HA = 8
N_WA = 16
GRID_ROWS = 32
GRID_COLS = 320
ROWS = 4
COLS = 20
PITCH = 24
WIDE = 26
HALF = 56
RING = 2 * 6 * PITCH


def normed(values, gain_vec, channels):
    inv_rms = lax.rsqrt(jnp.sum(values * values, axis=-1, keepdims=True) * (1.0 / channels) + 1e-06)
    half = values * inv_rms * (0.5 * gain_vec)
    return half + half * jnp.tanh(half)


def conv_frames(stores, w):
    total = None
    for a in range(3):
        lhs = jnp.concatenate([stores[a][...], stores[a + 1][...]], axis=0)
        part = jnp.dot(lhs, w[a], preferred_element_type=F32)
        total = part if total is None else total + part
    return total


def frame_pair(first, second):
    return jnp.concatenate([first.astype(F32), second.astype(F32)], axis=1)


def pack_rows(info, latent, cache, to_above, side):
    for f in range(2):
        for row in range(3):
            at = ((4 + f) * 3 + row) * COLS
            side[at : at + COLS] = cache[f, row].astype(F32)

    @pl.when(info[0] == 0)
    def _():
        for f in range(4):
            for row in range(3):
                at = (f * 3 + row) * COLS
                side[at : at + COLS] = latent[f, row].astype(F32)

    to_above[...] = side[...].astype(BF16)


def pack_caches(info, cache, fine, _, to_below, fine_up, side):
    @pl.when(info[0] == 1)
    def _():
        for f in range(2):
            for row in range(2):
                at = (f * 2 + row) * COLS
                side[at : at + COLS] = cache[f, 2 + row].astype(F32)
        side[80:120] = frame_pair(fine[0, 7], fine[1, 7])
        to_below[...] = side[...].astype(BF16)
        side[0:40] = frame_pair(fine[0, 0], fine[1, 0])
        fine_up[...] = side[0:48].astype(BF16)


def pack_columns(info, latent, cache, fine, below, above, under, left_0, right_0, left_1, right_1, far, side):
    far[0] = below[...].astype(F32)

    @pl.when(info[0] == 0)
    def _():
        for f in range(6):
            for row in range(1, 7):
                if row < ROWS:
                    line = (latent[f, row] if f < 4 else cache[f - 4, row]).astype(F32)
                    first, final = line[:3], line[17:20]
                else:
                    base = (f * 3 + row - ROWS) * COLS
                    first, final = far[0, base : base + 3], far[0, base + 17 : base + 20]
                at = (f * 6 + row - 1) * 3
                side[0, at : at + 3] = first
                side[1, at : at + 3] = final
        left_0[...] = side[0].astype(BF16)
        right_0[...] = side[1].astype(BF16)

    @pl.when(info[0] == 1)
    def _():
        far[1, 0:128] = above[...].astype(F32)
        far[1, 128:176] = under[...].astype(F32)
        for t in range(2):
            for u in range(8):
                if 2 <= u < 6:
                    line = cache[t, u - 2].astype(F32)
                    first, final = line[:2], line[18:20]
                else:
                    k, base = (1, (t * 2 + u) * COLS) if u < 2 else (0, ((4 + t) * 3 + u - 6) * COLS)
                    first, final = far[k, base : base + 2], far[k, base + 18 : base + 20]
                at = (t * 8 + u) * 2
                side[0, at : at + 2] = first
                side[1, at : at + 2] = final
        for e in range(10):
            if 1 <= e <= 8:
                line = frame_pair(fine[0, e - 1], fine[1, e - 1])
                first, final = line[0:1], line[39:40]
            else:
                k, base = (1, 80) if e == 0 else (1, 128)
                first, final = far[k, base : base + 1], far[k, base + 39 : base + 40]
            side[0, 32 + e : 33 + e] = first
            side[1, 32 + e : 33 + e] = final
        left_1[...] = side[0, 0:48].astype(BF16)
        right_1[...] = side[1, 0:48].astype(BF16)


def fold_weights(w_up_hbm, w_up, sem, out):
    copy = pltpu.make_async_copy(w_up_hbm, w_up, sem)
    copy.start()
    copy.wait()
    zeros = jnp.zeros((CM, 64), F32)
    taps = [jnp.transpose(w_up[k].astype(F32)) for k in range(9)]
    for br in range(2):
        for bc in range(2):
            place = br * 2 + bc
            for du in range(2):
                ps = ((0, 1), (2,))[du] if br == 0 else ((0,), (1, 2))[du]
                for dv in range(2):
                    qs = ((0, 1), (2,))[dv] if bc == 0 else ((0,), (1, 2))[dv]
                    total = None
                    for p in ps:
                        for q in qs:
                            part = taps[p * 3 + q]
                            total = part if total is None else total + part
                    both = jnp.concatenate([total, zeros], axis=1).astype(BF16)
                    out[(du * 2 + dv) * CM : (du * 2 + dv + 1) * CM, place * 256 : place * 256 + 256] = both


def first_section(group, info, latent, cache, below, left, right, w, b, g, out, kept, raw, act, side, far, patches):
    stores = [patches.at[0], patches.at[1], kept.at[0], kept.at[1]]
    if group == 1:
        stores = stores[2:] + stores[:2]
    last = info[1] == N_HA - 1
    side[0] = left[...].astype(F32)
    side[1] = right[...].astype(F32)
    far[...] = below[...].astype(F32)
    slots = [(1, False), (2, False), (3, False), (4, True), (3, True), (4, False), (5, False), (6, False)]
    for f in range(2 * group, 4):
        lead = group == 0 and f < 2
        frame = f if group == 1 else (4 + f if lead else f - 2)
        for slot, (row, hide) in enumerate(slots):
            if row >= ROWS:
                base = (frame * 3 + row - ROWS) * COLS
                line = far[base : base + COLS]
            else:
                line = (latent[frame, row] if frame < 4 else cache[frame - 4, row]).astype(F32)
            at = (frame * 6 + row - 1) * 3
            before = side[0, at : at + 3]
            after = side[1, at : at + 3]
            if hide:
                line, before, after = (jnp.where(last, 0.0, v) for v in (line, before, after))
            base = slot * WIDE
            raw[f, base : base + 3] = before
            raw[f, base + 3 : base + 3 + COLS] = line
            raw[f, base + 3 + COLS : base + WIDE] = after
        raw[f, 8 * WIDE : 216] = jnp.zeros((8, CM), F32)
        for lo in range(0, 216, 72):
            part = raw[f, lo : lo + 72]
            act[f, lo : lo + 72] = part if lead else normed(part, g[...], CM)
        for p in range(3):
            for q in range(3):
                top = p * WIDE + q
                low = top + 4 * WIDE
                both = jnp.concatenate([act[f, top : top + HALF], act[f, low : low + HALF]], axis=0)
                stores[f][:, (p * 3 + q) * CM : (p * 3 + q + 1) * CM] = both.astype(BF16)
    total = conv_frames(stores, w) + b[...]
    cols = lax.broadcasted_iota(jnp.int32, (PITCH, 1), 0) + (info[2] * COLS - 2)
    inside = (cols >= 0) & (cols < GRID_COLS)
    act[0, 0 : 2 * HALF] = total[: 2 * HALF]
    act[1, 0 : 2 * HALF] = total[2 * HALF :]
    for t in range(2):
        for r in range(4):
            src = (r // 2) * HALF + (r % 2) * WIDE
            res = ((r // 2) * 4 + r % 2 + 1) * WIDE + 1
            value = act[t, src : src + PITCH] + raw[2 + t, res : res + PITCH]
            out[t, r] = jnp.where(inside, value, 0.0).astype(BF16)


def first_early(info, latent, cache, below, left, right, w, b, g, out, kept, *scratch):
    @pl.when(info[0] == 0)
    def _():
        first_section(0, info, latent, cache, below, left, right, w, b, g, out, kept, *scratch)


def first_late(info, latent, below, left, right, kept, w, b, g, w_up_hbm, out, folded, *scratch):
    *scratch, w_up, sems = scratch

    @pl.when(info[0] == 0)
    def _():
        first_section(1, info, latent, None, below, left, right, w, b, g, out, kept, *scratch)

    @pl.when(info[0] == 1)
    def _():
        fold_weights(w_up_hbm, w_up, sems.at[0], folded)


def second_section(info, caches, tiles, w, b, g, out, kept, raw, act, side, far, patches):
    stores = [patches.at[0], patches.at[1], kept.at[0], kept.at[1]]
    if caches is None:
        stores = stores[2:] + stores[:2]
    first, last = info[1] == 0, info[1] == N_HA - 1
    if caches is not None:
        cache, below, above, under, left, right = caches
        far[1, 128:176] = under[...].astype(F32)
        side[0, 0:48] = left[...].astype(F32)
        side[1, 0:48] = right[...].astype(F32)
        far[0] = below[...].astype(F32)
        far[1, 0:128] = above[...].astype(F32)
    for f in range(0 if caches is not None else 2, 4):
        lead = caches is not None and f < 2
        t = f % 2
        for u in range(8):
            base = u * PITCH
            hide = first if u < 2 else (last if u > 5 else None)
            if lead:
                if 2 <= u < 6:
                    line = cache[t, u - 2].astype(F32)
                else:
                    k, at = (1, (t * 2 + u) * COLS) if u < 2 else (0, ((4 + t) * 3 + u - 6) * COLS)
                    line = far[k, at : at + COLS]
                at = (t * 8 + u) * 2
                before = side[0, at : at + 2]
                after = side[1, at : at + 2]
                if hide is not None:
                    line, before, after = (jnp.where(hide, 0.0, v) for v in (line, before, after))
                raw[f, base : base + 2] = before
                raw[f, base + 2 : base + 22] = line
                raw[f, base + 22 : base + 24] = after
            else:
                low, top = tiles
                line = (top[t, u] if u < 4 else low[t, u - 4]).astype(F32)
                raw[f, base : base + PITCH] = line if hide is None else jnp.where(hide, 0.0, line)
        raw[f, 8 * PITCH : 200] = jnp.zeros((8, CM), F32)
        for lo, hi in ((0, 96), (96, 200)):
            part = raw[f, lo:hi]
            act[f, lo:hi] = part if lead else normed(part, g[...], CM)
        for q in range(3):
            shifted = act[f, q : q + 192]
            for p in range(3):
                at = p * PITCH
                stores[f][:, (p * 3 + q) * CM : (p * 3 + q + 1) * CM] = shifted[at : at + 144].astype(BF16)
    total = conv_frames(stores, w) + b[...]
    cell = lax.broadcasted_iota(jnp.int32, (PITCH, 1), 0)
    cols = cell + (info[2] * COLS - 1)
    inside = (cols >= 0) & (cols < GRID_COLS) & (cell < 22)
    for t in range(2):
        for i in range(6):
            row_at = info[1] * ROWS - 1 + i
            fits = inside & (row_at >= 0) & (row_at < GRID_ROWS)
            res = (i + 1) * PITCH + 1
            at = t * 144 + i * PITCH
            value = total[at : at + PITCH] + raw[2 + t, res : res + PITCH]
            out[at : at + PITCH] = jnp.where(fits, value, 0.0).astype(BF16)


def second_early(info, cache, below, above, under, left, right, low, top, w, b, g, w_up_hbm, out, kept, folded, *scratch):
    *scratch, ring, w_up, sems = scratch

    @pl.when(info[0] == 1)
    def _():
        second_section(info, (cache, below, above, under, left, right), (low, top), w, b, g, out, kept, *scratch)
        first, last = info[1] == 0, info[1] == N_HA - 1
        side, far = scratch[2:4]
        ring[...] = jnp.zeros((112, CM), F32)
        for at, e, line, hide in ((0, 0, far[1, 80:120], first), (48, 9, far[1, 128:168], last)):
            ring[at : at + 1] = jnp.where(hide, 0.0, side[0, 32 + e : 33 + e])
            ring[at + 1 : at + 41] = jnp.where(hide, 0.0, line)
            ring[at + 41 : at + 42] = jnp.where(hide, 0.0, side[1, 32 + e : 33 + e])
        ring[96:104] = side[0, 33:41]
        ring[104:112] = side[1, 33:41]
        out[RING : RING + 112] = ring[...].astype(BF16)

    @pl.when(info[0] == 0)
    def _():
        fold_weights(w_up_hbm, w_up, sems.at[0], folded)


def second_late(info, low, top, kept, w, b, g, out, *scratch):
    @pl.when(info[0] == 1)
    def _():
        second_section(info, None, (low, top), w, b, g, out, kept, *scratch)


def last_section(info, lead, main, returned, cache, folded_0, folded_1, b_up, g, w_hbm, b,
                 out, coarse, ups, act, rows, ring, patches, wide, w, sems):
    copy = pltpu.make_async_copy(w_hbm, w.at[:, pl.ds(0, CF)], sems.at[0])
    copy.start()
    for k in range(27):
        w[k, CF:256] = jnp.zeros((64, CF), BF16)
    lanes = lambda ref: jnp.concatenate([ref[...], jnp.zeros((1, 64), F32)], axis=1)
    bias, gain = lanes(b_up), lanes(g)

    def upsample(src, w_up, slot, keep):
        for t in range(2):
            coarse[t, 0:144] = src[t * 144 : t * 144 + 144].astype(F32)
            coarse[t, 144:160] = jnp.zeros((16, CM), F32)
        lhs = [
            jnp.concatenate([coarse[t, du * PITCH + dv : du * PITCH + dv + 128].astype(BF16) for t in range(2)], axis=0)
            for du in range(2)
            for dv in range(2)
        ]
        lhs = jnp.concatenate(lhs, axis=1)
        cell = lax.broadcasted_iota(jnp.int32, (128, 1), 0)
        col = lax.rem(cell, PITCH)
        for phase in range(4):
            br, bc = phase // 2, phase % 2
            total = jnp.dot(lhs, w_up[:, phase * 256 : phase * 256 + 256], preferred_element_type=F32)
            value = (total + bias).astype(BF16).astype(F32)
            if br == 0:
                outside = (cell < PITCH) & (info[1] == 0)
            else:
                outside = (cell >= 4 * PITCH) & (info[1] == N_HA - 1)
            if bc == 0:
                outside |= (col == 0) & (info[2] == 0)
            else:
                outside |= (col == COLS) & (info[2] == N_WA - 1)
            unit = normed(value, gain, CF)
            for t in range(2):
                if keep:
                    ups[t, phase] = value[t * 128 : t * 128 + 128]
                act[slot + t, phase] = jnp.where(outside, 0.0, unit[t * 128 : t * 128 + 128])

    @pl.when(info[0] == 0)
    def _():
        rows[...] = jnp.zeros((2, 56, 128), F32)
        ring[...] = returned[RING : RING + 112].astype(F32)
        for t in range(2):
            part = slice(t * CF, t * CF + CF)
            for e in range(10):
                if e == 0 or e == 9:
                    at = 0 if e == 0 else 48
                    line = ring[at : at + 48][:, part]
                    rows[0, 0:48] = line[:, :128]
                    rows[1, 0:48, 0:64] = line[:, 128:]
                else:
                    line = cache[t, e - 1].astype(F32)
                    rows[0, 1:41] = line[:, :128]
                    rows[1, 1:41, 0:64] = line[:, 128:]
                    for at, col in ((95 + e, 0), (103 + e, 41)):
                        end = ring[at : at + 1][:, part]
                        rows[0, col : col + 1] = end[:, :128]
                        rows[1, col : col + 1, 0:64] = end[:, 128:]
                br, u = e % 2, e // 2
                for bc in range(2):
                    for c in range(2):
                        act[t, br * 2 + bc, u * PITCH : (u + 1) * PITCH, c * 128 : c * 128 + 128] = rows[
                            c, pl.ds(bc, PITCH, 2), :
                        ]
        upsample(returned, folded_0, 2, True)

    @pl.when(info[0] == 1)
    def _():
        upsample(lead, folded_1, 0, False)
        upsample(main, folded_1, 2, True)

    for f in range(4):
        for plane in range(4):
            for s in range(4):
                at = (s // 2) * PITCH + s % 2
                patches[f, plane * 4 + s] = act[f, plane, at : at + 96].astype(BF16)
    copy.wait()
    for yb in range(2):
        for xb in range(2):
            total = None
            blocks = [
                (((yb + p) % 2) * 2 + (xb + q) % 2) * 4 + ((yb + p) // 2) * 2 + (xb + q) // 2
                for p in range(3)
                for q in range(3)
            ]
            for a in range(3):
                lhs = jnp.concatenate([patches[a : a + 2, block].reshape(192, 256) for block in blocks], axis=1)
                taps = w[a * 9 : a * 9 + 9].reshape(9 * 256, CF)
                part = jnp.dot(lhs, taps, preferred_element_type=F32)
                total = part if total is None else total + part
            total = total + b[...]
            plane = ((yb + 1) % 2) * 2 + (xb + 1) % 2
            at = ((yb + 1) // 2) * PITCH + (xb + 1) // 2
            for t in range(2):
                value = total[t * 96 : t * 96 + 96] + ups[t, plane, at : at + 96][:, :CF]
                for y in range(4):
                    line = value[y * PITCH : y * PITCH + COLS]
                    wide[0, t, 2 * y + yb, pl.ds(xb, COLS, 2), :] = line[:, :128]
                    wide[1, t, 2 * y + yb, pl.ds(xb, COLS, 2), :] = jnp.concatenate(
                        [line[:, 128:], line[:, 128:]], axis=1
                    )
    for t in range(2):
        for y in range(8):
            out[t, y, :, :128] = wide[0, t, y].astype(BF16)
            out[t, y, :, 128:] = wide[1, t, y][:, :64].astype(BF16)


VMEM = pl.BlockSpec(memory_space=pltpu.VMEM)
SMEM = pl.BlockSpec(memory_space=pltpu.SMEM)
HBM = pl.BlockSpec(memory_space=pltpu.HBM)


def call(body, specs, outs, scratch, *operands, flops=0, megabytes=20):
    kinds = {"s": SMEM, "v": VMEM, "h": HBM}
    return pl.pallas_call(
        body,
        out_shape=[jax.ShapeDtypeStruct(shape, BF16) for shape in outs],
        in_specs=[kinds[c] for c in specs],
        out_specs=[VMEM] * len(outs),
        scratch_shapes=scratch,
        compiler_params=pltpu.CompilerParams(vmem_limit_bytes=megabytes * 2**20),
        cost_estimate=pl.CostEstimate(flops=flops, bytes_accessed=2**20, transcendentals=0),
    )(*operands)


def device_at(s, h, w):
    return (s * N_HA + h) * N_WA + w


def pairs_between(src_seg, dst_seg, dh, dw, wrap=False):
    pairs = []
    for h in range(N_HA):
        for w in range(N_WA):
            if (wrap or 0 <= h - dh < N_HA) and 0 <= w - dw < N_WA:
                pairs.append((device_at(src_seg, (h - dh) % N_HA, w - dw), device_at(dst_seg, h, w)))
    return pairs


def shards(latent, w_mid, b_mid, g_mid, cache_mid, w_up, b_up, g_fine, cache_fine, w_fine, b_fine):
    info = jnp.stack([lax.axis_index(axis) for axis in AXES]).astype(jnp.int32)
    kernel = w_mid.reshape(3, 9 * CM, CM)
    up_kernel = jnp.swapaxes(w_up, 2, 3).reshape(9, CF, CM)
    dma = pltpu.SemaphoreType.DMA

    cache = cache_mid[0]
    side = pltpu.VMEM((2, 112, CM), F32)
    far = lambda count: pltpu.VMEM((count, 368, CM) if count > 1 else (368, CM), F32)
    (to_above,) = call(pack_rows, "svv", [(368, CM)], [far(1)], info, latent, cache, megabytes=3)
    below = lax.ppermute(to_above, "ha", [(i, (i - 1) % N_HA) for i in range(N_HA)])
    to_below, fine_up = call(
        pack_caches, "svvv", [(128, CM), (48, CM)], [pltpu.VMEM((128, CM), F32)], info, cache, cache_fine, to_above,
        megabytes=3,
    )
    above = lax.ppermute(to_below, AXES, pairs_between(1, 1, 1, 0))
    under = lax.ppermute(fine_up, AXES, pairs_between(1, 1, -1, 0))
    sides = call(
        pack_columns, "svvvvvv", [(112, CM)] * 2 + [(48, CM)] * 2, [far(2), side],
        info, latent, cache, cache_fine, below, above, under, megabytes=3, flops=2 * 10**9,
    )
    right_0, left_0 = (lax.ppermute(sides[k], AXES, pairs_between(0, 0, 0, 2 * k - 1)) for k in range(2))
    right_1, left_1 = (lax.ppermute(sides[2 + k], AXES, pairs_between(1, 1, 0, 2 * k - 1)) for k in range(2))

    up_scratch = [pltpu.VMEM((9, CF, CM), BF16), dma((1,))]
    folded_shape = (4 * CM, 1024)
    first_scratch = [
        pltpu.VMEM((4, 216, CM), F32),
        pltpu.VMEM((4, 216, CM), F32),
        side,
        far(1),
        pltpu.VMEM((2, 2 * HALF, 9 * CM), BF16),
    ]
    first_shape = (2, ROWS, PITCH, CM)
    first_flops = 2 * 224 * 27 * CM * CM
    spread = lambda tile: [lax.ppermute(tile, AXES, pairs_between(0, 1, dh, 0, True)) for dh in range(2)]
    early, kept = call(
        first_early, "svvvvvvvv", [first_shape, (2, 2 * HALF, 9 * CM)], first_scratch,
        info, latent, cache, below, left_0, right_0, kernel, b_mid, g_mid, flops=first_flops, megabytes=16,
    )
    group_a = spread(early)
    late, folded_1 = call(
        first_late, "svvvvvvvvh", [first_shape, folded_shape], first_scratch + up_scratch,
        info, latent, below, left_0, right_0, kept, kernel, b_mid, g_mid, up_kernel, flops=first_flops, megabytes=16,
    )
    group_b = spread(late)

    second_scratch = [
        pltpu.VMEM((4, 200, CM), F32),
        pltpu.VMEM((4, 200, CM), F32),
        side,
        far(2),
        pltpu.VMEM((2, 144, 9 * CM), BF16),
    ]
    second_flops = 2 * 288 * 27 * CM * CM
    second_a, kept, folded_0 = call(
        second_early, "svvvvvvvvvvvh", [(RING + 112, CM), (2, 144, 9 * CM), folded_shape],
        second_scratch + [pltpu.VMEM((112, CM), F32)] + up_scratch,
        info, cache, below, above, under, left_1, right_1, *group_a, kernel, b_mid, g_mid, up_kernel, flops=second_flops, megabytes=16,
    )
    returned = lax.ppermute(second_a, "segment", [(1, 0)])
    (second_b,) = call(
        second_late, "svvvvvv", [(RING, CM)], second_scratch,
        info, *group_b, kept, kernel, b_mid, g_mid, flops=second_flops, megabytes=16,
    )
    (decoded,) = call(
        last_section, "svvvvvvvvhv", [(2, 8, 40, CF)],
        [
            pltpu.VMEM((2, 160, CM), F32),
            pltpu.VMEM((2, 4, 128, 256), F32),
            pltpu.VMEM((4, 4, 128, 256), F32),
            pltpu.VMEM((2, 56, 128), F32),
            pltpu.VMEM((112, CM), F32),
            pltpu.VMEM((4, 16, 96, 256), BF16),
            pltpu.VMEM((2, 2, 8, 40, 128), F32),
            pltpu.VMEM((27, 256, CF), BF16),
            dma((1,)),
        ],
        info, second_a, second_b, returned, cache_fine, folded_0, folded_1,
        b_up[None], g_fine[None], w_fine.reshape(27, CF, CF), b_fine[None],
        flops=2 * 768 * 27 * CF * CF, megabytes=16,
    )
    return decoded


def solution(mesh):
    return jax.shard_map(
        shards,
        mesh=mesh,
        in_specs=(
            P(None, "ha", "wa", None),
            P("segment", None, None, None, None, None),
            P("segment", None),
            P("segment", None),
            P("segment", None, "ha", "wa", None),
            P(),
            P(),
            P(),
            P(None, "ha", "wa", None),
            P(),
            P(),
        ),
        out_specs=P("segment", "ha", "wa", None),
        check_vma=False,
    )
```
